32 devices in a mesh: seq: 16 (over z, y, x), tp: 2 (over core).
Axes of the slice: x: 2, y: 2, z: 4, core: 2. Of those that a mesh axis runs over, the one named last changes fastest.
Arguments:
- cache_keys: bfloat16 [32768, 2048], P('seq', 'tp'), may hold values from -13 to 13
- cache_values: bfloat16 [32768, 2048], P('seq', 'tp'), may hold values from -12 to 12
- keep_flags: int32 [32768], P('seq'), may hold values from 0 to 1, as said below
- drop_weight: int32 [32768], P('seq'), may hold values from 1 to 255
- req_blocks: int32 [12], replicated, may hold values from 1 to 32, 256 in all
- queries: bfloat16 [12, 2048], P(None, 'tp'), may hold values from -48 to 48
- new_keys: bfloat16 [12, 2048], P(None, 'tp'), may hold values from -12 to 12
- new_values: bfloat16 [12, 2048], P(None, 'tp'), may hold values from -12 to 12
- out_weight: bfloat16 [2048, 2048], P('tp', 'seq'), may hold values from -0.125 to 0.125
Outputs:
- packed_keys: bfloat16 [16640, 2048], P('seq', 'tp')
- packed_values: bfloat16 [16640, 2048], P('seq', 'tp')
- packed_bias: bfloat16 [16640], P('seq')
- packed_request: int32 [16640], P('seq')
- layer_output: bfloat16 [12, 2048], P('tp', 'seq')
The draws below stay inside these ranges and needn't reach their ends.
Inputs may be any that keep to these rules, and one draw needn't show every extreme that they name: `keep_flags`: every aligned block of 128 rows keeps between 32 and 64 rows; in every draw all blocks of the rows of some one index of seq keep exactly 64. `req_blocks`: the entries sum to 256; the largest is 32.
All inputs are finite; a program needn't handle non-finite values.
Results may differ from the reference program's by a relative error of at most 0.009.
Values may be sent and summed in bfloat16 or wider, within the bound.
No kernel may reach another device: no remote copies, remote signals or barrier semaphores. Data moves between devices by JAX's collectives and lax.ppermute only.
A program may use at most 64 MiB of HBM per device.

```python
import math
import jax
import jax.numpy as jnp
import numpy as np
from jax import lax

D = 2048
HEADS = 8
HD = 256
BLOCK = 128
ROWS_DEV = 2048
REQS = 12
ROWS = 32768
TOTAL_BLOCKS = 256
LONG_BLOCKS = 32
K_DEV = 1040
SLOTS = 16640
N_SEQ = 16


def shared_direction(key):
    signs = jax.random.normal(jax.random.fold_in(key, 7), (D,), jnp.float32)
    return jnp.where(signs >= 0.0, 2.0, -2.0).astype(jnp.float32)


def draw_cache_keys(key, part):
    drawn = jnp.clip(2.0 * jax.random.normal(jax.random.fold_in(key, 11), (ROWS, D), jnp.float32), -12.0, 12.0)
    direction = shared_direction(key)
    positions = jnp.arange(ROWS, dtype=jnp.int32)
    marked = positions % 97 == 0
    factor = 1.0 + 0.01 * (positions // 97 % 8).astype(jnp.float32)
    drawn = jnp.where(marked[:, None], direction[None, :] * factor[:, None], drawn)
    return drawn.astype(jnp.bfloat16)


def draw_queries(key, part):
    drawn = jnp.clip(jax.random.normal(jax.random.fold_in(key, 13), (REQS, D), jnp.float32), -6.0, 6.0)
    direction = shared_direction(key)
    chosen = jax.random.bernoulli(jax.random.fold_in(key, 17), 0.5, (REQS,))
    strength = jax.random.uniform(jax.random.fold_in(key, 19), (REQS,), jnp.float32, 25.0, 45.0)
    aligned = direction[None, :] * (strength / jnp.sqrt(jnp.float32(HD)))[:, None]
    drawn = jnp.where(chosen[:, None], aligned, drawn)
    return drawn.astype(jnp.bfloat16)


def draw_keep_flags(key, part):
    block_count = ROWS // BLOCK
    counts = jax.random.randint(jax.random.fold_in(key, 23), (block_count,), BLOCK // 4, BLOCK // 2 + 1)
    full_device = jax.random.randint(jax.random.fold_in(key, 29), (), 0, ROWS // ROWS_DEV)
    block_device = jnp.arange(block_count, dtype=jnp.int32) // (ROWS_DEV // BLOCK)
    counts = jnp.where(block_device == full_device, BLOCK // 2, counts)
    noise = jax.random.randint(jax.random.fold_in(key, 31), (block_count, BLOCK), 0, 2 ** 20)
    ranked = noise * BLOCK + jnp.arange(BLOCK, dtype=jnp.int32)[None, :]
    order = jnp.argsort(ranked, axis=1)
    position_rank = jnp.argsort(order, axis=1)
    return (position_rank < counts[:, None]).astype(jnp.int32).reshape(ROWS)


def set_ends(drawn, stream_key, low, top_value):
    spot = [jax.random.randint(jax.random.fold_in(stream_key, axis), (), 0, length) for axis, length in enumerate(drawn.shape)]
    widest = drawn.shape.index(max(drawn.shape))
    neighbour = spot[:widest] + [(spot[widest] + 1) % drawn.shape[widest]] + spot[widest + 1:]
    return drawn.at[tuple(spot)].set(low).at[tuple(neighbour)].set(top_value)


def block_scale(key, dims, cuts, smallest, largest):
    factor_of = 1.0
    for axis_at, blocks in cuts:
        draws = jax.random.uniform(jax.random.fold_in(jax.random.fold_in(key, 6), axis_at), (blocks,), jnp.float32, smallest / len(cuts), largest / len(cuts))
        factor_of = factor_of * jnp.repeat(jnp.exp(draws), dims[axis_at] // blocks).reshape((-1,) + (1,) * (len(dims) - 1 - axis_at))
    return factor_of


def profile(number_of, total, most, slope):
    weights = [(1 << 20) // math.isqrt(grade ** slope) + 1 for grade in range(2, number_of + 1)]
    spare, given = total - most - (number_of - 1), [1] * (number_of - 1)
    while spare > 0:
        movable = [i for i in range(number_of - 1) if given[i] < most]
        whole, left = sum([weights[i] for i in movable]), spare
        for i in movable:
            more = min(most - given[i], max(1, left * weights[i] // whole), spare)
            given[i] = given[i] + more
            spare = spare - more
    return np.array([most] + given)


def uneven(own_key, count, total, bound, lean):
    if count == 2:
        one = jax.random.randint(own_key, (), max(1, total - bound), min(bound, total - 1) + 1)
        return jnp.stack([one, total - one])
    lengths = jnp.asarray(profile(count, total, bound, lean), jnp.int32)
    twos = (count - 1) // 2
    source_of, receiver = lengths[1:1 + 2 * twos:2], lengths[2:2 + 2 * twos:2]
    margin = jnp.minimum(source_of - 1, bound - receiver)
    shifted = jax.random.randint(jax.random.fold_in(own_key, 1), (twos,), 0, 1 << 20) % (margin + 1)
    lengths = lengths.at[1:1 + 2 * twos:2].set(source_of - shifted).at[2:2 + 2 * twos:2].set(receiver + shifted)
    return lengths[jax.random.permutation(jax.random.fold_in(own_key, 2), count)]


def gaussian(own_key, dims, spread, bound, cuts=(), kind=jnp.bfloat16):
    factor_of = block_scale(own_key, dims, cuts, -0.22, 0.18) if cuts else 1.0
    array = jax.random.normal(own_key, dims, jnp.float32) * spread * factor_of
    return jnp.minimum(jnp.maximum(array, -bound), bound).astype(kind)


def setup_inputs(seed: int = 0) -> dict:
    arg_keys = jax.random.split(jax.random.key(seed), 10)
    return {
        "cache_keys": draw_cache_keys(jax.random.fold_in(arg_keys[9], 71), 0),
        "cache_values": gaussian(arg_keys[1], (ROWS, D), 2.0, 12.0, ((0, 16), (1, 2))),
        "keep_flags": draw_keep_flags(jax.random.fold_in(arg_keys[9], 71), 0),
        "drop_weight": set_ends(jax.random.randint(arg_keys[3], (ROWS,), 1, 256), jax.random.fold_in(arg_keys[3], 1), 1, 255).astype(jnp.int32),
        "req_blocks": uneven(arg_keys[4], REQS, TOTAL_BLOCKS, LONG_BLOCKS, 2).astype(jnp.int32),
        "queries": draw_queries(jax.random.fold_in(arg_keys[9], 71), 0),
        "new_keys": gaussian(arg_keys[6], (REQS, D), 2.0, 12.0, ((1, 2),)),
        "new_values": gaussian(arg_keys[7], (REQS, D), 2.0, 12.0, ((1, 2),)),
        "out_weight": gaussian(arg_keys[8], (D, D), D ** -0.5, 0.125, ((0, 2), (1, 16))),
    }


def fold_cache(cache, keep_flags, drop_weight):
    blocks_dev = ROWS_DEV // BLOCK
    weights = (drop_weight * (1 - keep_flags)).astype(jnp.float32).reshape(N_SEQ, blocks_dev, BLOCK)
    pieces = cache.reshape(N_SEQ, blocks_dev, BLOCK, cache.shape[1])

    def one_group(operands):
        group_weights, group_rows = operands
        summed = jnp.einsum('bi,bid->bd', group_weights, group_rows.astype(jnp.float32), precision=lax.Precision.HIGHEST)
        return summed / lax.optimization_barrier(jnp.sum(group_weights, axis=1))[:, None]
    folded = lax.map(one_group, (weights, pieces))
    return folded.reshape(-1, cache.shape[1]).astype(jnp.bfloat16)

def reference(cache_keys, cache_values, keep_flags, drop_weight, req_blocks, queries, new_keys, new_values, out_weight):
    block_count = ROWS // BLOCK
    keep_blocks = keep_flags.reshape(block_count, BLOCK)
    kept_count = lax.optimization_barrier(jnp.sum(keep_blocks, axis=1)).astype(jnp.int32)
    within = (jnp.cumsum(keep_blocks, axis=1) - keep_blocks).astype(jnp.int32)
    block_size = kept_count + 1
    block_base = (jnp.cumsum(block_size) - block_size).astype(jnp.int32)
    request_ends = jnp.cumsum(req_blocks).astype(jnp.int32)
    block_index = jnp.arange(block_count, dtype=jnp.int32)
    block_request = lax.optimization_barrier(jnp.sum((block_index[:, None] >= request_ends[None, :]).astype(jnp.int32), axis=1)).astype(jnp.int32)
    slot_count = SLOTS
    row_rank = (block_base[:, None] + within).reshape(-1)
    fold_rank = block_base + kept_count

    def place(global_rank):
        return (global_rank % N_SEQ * K_DEV + global_rank // N_SEQ).astype(jnp.int32)
    row_slot = jnp.where(keep_flags == 1, place(row_rank), slot_count).astype(jnp.int32)
    fold_slot = place(fold_rank)
    folded_keys = fold_cache(cache_keys, keep_flags, drop_weight)
    folded_values = fold_cache(cache_values, keep_flags, drop_weight)
    folded_bias = jnp.log((BLOCK - kept_count).astype(jnp.float32)).astype(jnp.bfloat16)
    packed_keys = jnp.zeros((slot_count, D), jnp.bfloat16).at[row_slot].set(cache_keys, mode='drop').at[fold_slot].set(folded_keys)
    packed_values = jnp.zeros((slot_count, D), jnp.bfloat16).at[row_slot].set(cache_values, mode='drop').at[fold_slot].set(folded_values)
    packed_bias = jnp.zeros((slot_count,), jnp.bfloat16).at[fold_slot].set(folded_bias)
    row_request = jnp.repeat(block_request, BLOCK)
    packed_request = jnp.full((slot_count,), -1, jnp.int32).at[row_slot].set(row_request, mode='drop').at[fold_slot].set(block_request)
    score_scale = 1.0 / jnp.sqrt(jnp.float32(HD))
    request_index = jnp.arange(REQS, dtype=jnp.int32)
    member = packed_request[None, :] == request_index[:, None]
    bias_row = packed_bias.astype(jnp.float32)[None, :]
    outputs = []
    for head_index in range(HEADS):
        lower = head_index * HD
        head_query = queries[:, lower:lower + HD]
        head_keys = packed_keys[:, lower:lower + HD]
        head_values = packed_values[:, lower:lower + HD]
        scores = jnp.dot(head_query, head_keys.T, preferred_element_type=jnp.float32) * score_scale + bias_row
        scores = jnp.where(member, scores, jnp.float32(-1e+30))
        own_score = lax.optimization_barrier(jnp.sum(head_query.astype(jnp.float32) * new_keys[:, lower:lower + HD].astype(jnp.float32), axis=1)) * score_scale
        peak = jnp.maximum(lax.optimization_barrier(jnp.max(scores, axis=1)), own_score)
        probs = jnp.where(member, jnp.exp(scores - peak[:, None]), jnp.float32(0.0))
        own_prob = jnp.exp(own_score - peak)
        total = lax.optimization_barrier(jnp.sum(probs, axis=1)) + own_prob
        weighted = jnp.dot(probs.astype(jnp.bfloat16), head_values, preferred_element_type=jnp.float32)
        weighted = weighted + own_prob[:, None] * new_values[:, lower:lower + HD].astype(jnp.float32)
        outputs.append(weighted / total[:, None])
    attention = jnp.concatenate(outputs, axis=1).astype(jnp.bfloat16)
    layer_output = jnp.dot(attention, out_weight, preferred_element_type=jnp.float32).astype(jnp.bfloat16)
    return (packed_keys, packed_values, packed_bias, packed_request, layer_output)
```

```python
import functools

import jax
import jax.numpy as jnp
from jax import lax
from jax.experimental import pallas as pl
from jax.experimental.pallas import tpu as pltpu
from jax.sharding import PartitionSpec as P

HD = 256
BLOCK = 128
LANES = 128
SUB = 16
LEAST_KEPT = BLOCK // 4
MOST_KEPT = BLOCK // 2
LOW = -1e30
VMEM_LIMIT = 56 * 1024 * 1024


class Geometry:
    def __init__(self, peers, blocks, features):
        self.peers = peers
        self.blocks = blocks
        self.features = features
        self.heads = features // HD
        self.slots = blocks * (MOST_KEPT + 1)
        self.peer_rows = -(-self.slots // peers)
        self.groups = self.peer_rows // SUB
        self.main = self.groups * SUB
        self.chunks = 2 * features // LANES
        self.tail = -(-self.chunks // SUB) * SUB
        self.slab = self.chunks * self.main + self.tail
        self.group_rows = SUB * peers
        assert self.peer_rows == self.main + 1
        self.join = min(peers, max(1, 256 // self.main))
        self.joins = peers // self.join
        window = self.join * self.peer_rows + SUB - 1
        self.window = min(-(-window // SUB) * SUB, self.slots)
        assert self.slots % SUB == 0 and peers % self.join == 0

    def block_range(self, first, last):
        low = max(0, -(-(first - MOST_KEPT) // (MOST_KEPT + 1)))
        high = min(self.blocks - 1, last // (LEAST_KEPT + 1))
        return low, high + 1


def iota(shape, axis):
    return lax.broadcasted_iota(jnp.int32, shape, axis)


def dot(a, b, contract=((1,), (0,))):
    return lax.dot_general(a, b, (contract, ((), ())), preferred_element_type=jnp.float32)


def pack_kernel(
    geo, keep_ref, weight_ref, first_ref, last_ref, query_ref, key_ref, value_ref,
    packed_ref, part_ref, pick_ref, scale_ref, fold_ref, left_ref,
):
    step = pl.program_id(0)
    blocks, peers = geo.blocks, geo.peers
    ranges = [
        geo.block_range(g * geo.group_rows, (g + 1) * geo.group_rows - 1) for g in range(geo.groups)
    ]
    places = []
    place = 0
    for low, high in ranges:
        places.append(place)
        place += (high - low) * BLOCK
    tail_low, tail_high = geo.block_range(geo.main * peers, geo.slots - 1)
    tail_place = place

    keep = keep_ref[...].astype(jnp.float32)
    kept = jnp.sum(keep, axis=1, keepdims=True)
    dropped = weight_ref[...].astype(jnp.float32) * (1.0 - keep)
    inverse = 1.0 / jnp.sum(dropped, axis=1, keepdims=True)

    @pl.when(step == 0)
    def _():
        earlier = (iota((BLOCK, BLOCK), 0) < iota((BLOCK, BLOCK), 1)).astype(jnp.bfloat16)
        within = dot(keep.astype(jnp.bfloat16), earlier)
        before = (iota((blocks, blocks), 1) < iota((blocks, blocks), 0)).astype(jnp.bfloat16)
        sizes = jnp.broadcast_to(kept + 1.0, (blocks, BLOCK)).astype(jnp.bfloat16)
        base = dot(before, sizes)
        entry = jnp.where(keep > 0.0, base + within, -1.0).astype(jnp.int32)
        fold_entry = (base + kept).astype(jnp.int32)

        def select(index, low, high, rows, place):
            scale = jnp.ones((rows, BLOCK), jnp.float32)
            for b in range(low, high):
                folds = index == fold_entry[b : b + 1, :]
                one = jnp.where(index == entry[b : b + 1, :], 1.0, 0.0)
                picked = jnp.where(folds, dropped[b : b + 1, :], one)
                at = place + (b - low) * BLOCK
                pick_ref[0:rows, at : at + BLOCK] = picked.astype(jnp.bfloat16)
                scale = jnp.where(folds, inverse[b : b + 1, :], scale)
            return scale

        rows = geo.group_rows
        row, col = iota((rows, BLOCK), 0), 0
        for g in range(geo.groups):
            index = (g * SUB + row % SUB) * peers + row // SUB
            scale_ref[g, :, :] = select(index, *ranges[g], rows, places[g])
        index = geo.main * peers + iota((peers, BLOCK), 0)
        scale_ref[geo.groups, 0:peers, :] = select(index, tail_low, tail_high, peers, tail_place)
        for b in range(blocks):
            mine = iota((blocks, BLOCK), 0) == b
            fold_ref[:, b * BLOCK : (b + 1) * BLOCK] = jnp.where(
                mine, dropped[b : b + 1, :], 0.0
            ).astype(jnp.bfloat16)

    for part, source in enumerate((key_ref, value_ref)):
        for g in range(geo.groups):
            low, high = ranges[g]
            rows = dot(
                pick_ref[:, places[g] : places[g] + (high - low) * BLOCK],
                source[low * BLOCK : high * BLOCK, :],
            )
            for half in range(HD // LANES):
                chunk = rows[:, half * LANES : (half + 1) * LANES] * scale_ref[g]
                chunk = chunk.astype(jnp.bfloat16).reshape(peers, SUB, LANES)
                at = pl.multiple_of(
                    (step * 4 + part * 2 + half) * geo.main + g * SUB, SUB
                )
                packed_ref[:, pl.ds(at, SUB), :] = chunk
        tail = dot(
            pick_ref[0:peers, tail_place : tail_place + (tail_high - tail_low) * BLOCK],
            source[tail_low * BLOCK : tail_high * BLOCK, :],
        )
        for half in range(HD // LANES):
            chunk = tail[:, half * LANES : (half + 1) * LANES] * scale_ref[geo.groups, 0:peers, :]
            at = pl.multiple_of((step * 4 + part * 2 + half) * peers, SUB)
            left_ref[pl.ds(at, peers), :] = chunk.astype(jnp.bfloat16)

    @pl.when(step == geo.heads - 1)
    def _():
        shape = (peers * geo.tail, geo.chunks * peers)
        row, col = iota(shape, 0), iota(shape, 1)
        wanted = row % geo.tail * peers + row // geo.tail
        turn = jnp.where(wanted == col, 1.0, 0.0).astype(jnp.bfloat16)
        tails = dot(turn, left_ref[...]).astype(jnp.bfloat16).reshape(peers, geo.tail, LANES)
        packed_ref[:, geo.chunks * geo.main :, :] = tails

    query = query_ref[...]
    first, last = first_ref[...], last_ref[...]
    requests = query.shape[0]
    score_scale = HD**-0.5
    folded_keys = (dot(fold_ref[...], key_ref[...]) * inverse).astype(jnp.bfloat16)
    folded_values = (dot(fold_ref[...], value_ref[...]) * inverse).astype(jnp.bfloat16)
    ones = jnp.ones((8, BLOCK), jnp.bfloat16)
    kept_lanes = dot(ones, keep.astype(jnp.bfloat16), ((1,), (1,)))[0:1, :]
    bias = jnp.log(BLOCK - kept_lanes).astype(jnp.bfloat16).astype(jnp.float32)
    fold_scores = dot(query, folded_keys, ((1,), (1,))) * score_scale + bias
    block = iota((requests, blocks), 1)
    fold_member = (block >= first) & (block < last)
    fold_scores = jnp.where(fold_member, fold_scores, LOW)
    scores = dot(query, key_ref[...], ((1,), (1,))) * score_scale
    lane_block = iota((requests, blocks * BLOCK), 1) // BLOCK
    kept_rows = jnp.concatenate(
        [jnp.broadcast_to(keep[b : b + 1, :], (requests, BLOCK)) for b in range(blocks)], axis=1
    )
    member = (lane_block >= first) & (lane_block < last) & (kept_rows > 0.0)
    scores = jnp.where(member, scores, LOW)
    peak = jnp.maximum(
        jnp.max(scores, axis=1, keepdims=True), jnp.max(fold_scores, axis=1, keepdims=True)
    )
    probs = jnp.where(member, jnp.exp(scores - peak), 0.0)
    fold_probs = jnp.where(fold_member, jnp.exp(fold_scores - peak), 0.0)
    total = jnp.sum(probs, axis=1, keepdims=True) + jnp.sum(fold_probs, axis=1, keepdims=True)
    mixed = dot(probs.astype(jnp.bfloat16), value_ref[...]) + dot(
        fold_probs.astype(jnp.bfloat16), folded_values
    )
    part_ref[0, :, 0:HD] = mixed
    part_ref[0, :, HD:] = jnp.where(iota((requests, LANES), 1) < LANES // 2, peak, total)


def pack(geo, keep, weight, first, last, queries, cache_keys, cache_values):
    rows = cache_keys.shape[0]
    requests = queries.shape[0]
    width = 0
    for g in range(geo.groups):
        low, high = geo.block_range(g * geo.group_rows, (g + 1) * geo.group_rows - 1)
        width += (high - low) * BLOCK
    low, high = geo.block_range(geo.main * geo.peers, geo.slots - 1)
    width += (high - low) * BLOCK
    whole = lambda *shape: pl.BlockSpec(shape, lambda t: (0,) * len(shape))
    return pl.pallas_call(
        functools.partial(pack_kernel, geo),
        grid=(geo.heads,),
        in_specs=[
            whole(geo.blocks, BLOCK),
            whole(geo.blocks, BLOCK),
            whole(requests, 1),
            whole(requests, 1),
            pl.BlockSpec((requests, HD), lambda t: (0, t)),
            pl.BlockSpec((rows, HD), lambda t: (0, t)),
            pl.BlockSpec((rows, HD), lambda t: (0, t)),
        ],
        out_specs=[
            whole(geo.peers, geo.slab, LANES),
            pl.BlockSpec((1, requests, HD + LANES), lambda t: (t, 0, 0)),
        ],
        out_shape=[
            jax.ShapeDtypeStruct((geo.peers, geo.slab, LANES), jnp.bfloat16),
            jax.ShapeDtypeStruct((geo.heads, requests, HD + LANES), jnp.float32),
        ],
        scratch_shapes=[
            pltpu.VMEM((geo.group_rows, width), jnp.bfloat16),
            pltpu.VMEM((geo.groups + 1, geo.group_rows, BLOCK), jnp.float32),
            pltpu.VMEM((geo.blocks, rows), jnp.bfloat16),
            pltpu.VMEM((geo.chunks * geo.peers, LANES), jnp.bfloat16),
        ],
        compiler_params=pltpu.CompilerParams(vmem_limit_bytes=VMEM_LIMIT),
        cost_estimate=pl.CostEstimate(
            flops=2 * geo.group_rows * width * 2 * geo.features,
            bytes_accessed=3 * rows * geo.features * 2,
            transcendentals=0,
        ),
    )(keep, weight, first, last, queries, cache_keys, cache_values)


def turn_kernel(geo, start_ref, packed_ref, sent_ref, sems):
    start = start_ref[0]
    copies = []
    for d in range(geo.peers):
        group = lax.rem(d + geo.peers - start, geo.peers)
        copies.append(pltpu.make_async_copy(packed_ref.at[group], sent_ref.at[d], sems.at[d]))
    for copy in copies:
        copy.start()
    for copy in copies:
        copy.wait()


def turn(geo, start, packed):
    return pl.pallas_call(
        functools.partial(turn_kernel, geo),
        in_specs=[pl.BlockSpec(memory_space=pltpu.SMEM), pl.BlockSpec(memory_space=pl.ANY)],
        out_specs=pl.BlockSpec(memory_space=pl.ANY),
        out_shape=jax.ShapeDtypeStruct(packed.shape, packed.dtype),
        scratch_shapes=[pltpu.SemaphoreType.DMA((geo.peers,))],
        cost_estimate=pl.CostEstimate(flops=0, bytes_accessed=2 * packed.size * 2, transcendentals=0),
    )(start, packed)


def unpack_kernel(geo, slot_ref, slab_ref, tail_ref, keys_ref, values_ref, pick_ref, tails_ref):
    step = pl.program_id(0)
    peers, main = geo.peers, geo.main
    width = geo.join * main
    lows = []
    for q in range(geo.joins):
        low = jnp.minimum(slot_ref[q * geo.join] // SUB * SUB, geo.slots - geo.window)
        lows.append(pl.multiple_of(low, SUB))

    @pl.when(step == 0)
    def _():
        for q in range(geo.joins):
            lane = iota((1, width), 1)
            target = lane % main
            last = iota((1, peers), 1) * 0 - 1
            for j in range(geo.join):
                at = slot_ref[q * geo.join + j] - lows[q]
                target = target + jnp.where(lane // main == j, at, 0)
                last = jnp.where(iota((1, peers), 1) == q * geo.join + j, at + main, last)
            picked = jnp.where(iota((geo.window, width), 0) == target, 1.0, 0.0)
            pick_ref[q, :, 0:width] = picked.astype(jnp.bfloat16)
            picked = jnp.where(iota((geo.window, peers), 0) == last, 1.0, 0.0)
            pick_ref[q, :, width : width + peers] = picked.astype(jnp.bfloat16)
        shape = (geo.chunks * peers, peers * geo.tail)
        row, col = iota(shape, 0), iota(shape, 1)
        wanted = row % peers * geo.tail + row // peers
        back = jnp.where(wanted == col, 1.0, 0.0).astype(jnp.bfloat16)
        tails = tail_ref[...].reshape(peers * geo.tail, LANES)
        tails_ref[...] = dot(back, tails).astype(jnp.bfloat16)

    for part, out_ref in enumerate((keys_ref, values_ref)):
        out_ref[...] = jnp.zeros_like(out_ref)
        halves = [part * 2 + half for half in range(HD // LANES)]
        tails = jnp.concatenate(
            [tails_ref[pl.ds(pl.multiple_of((step * 4 + c) * peers, SUB), peers), :] for c in halves],
            axis=1,
        )
        for q in range(geo.joins):
            rows = jnp.concatenate(
                [
                    slab_ref[
                        q * geo.join : (q + 1) * geo.join, c * main : (c + 1) * main, :
                    ].reshape(width, LANES)
                    for c in halves
                ],
                axis=1,
            )
            placed = dot(pick_ref[q, :, 0:width], rows)
            placed = placed + dot(pick_ref[q, :, width : width + peers], tails)
            out_ref[pl.ds(lows[q], geo.window), :] += placed.astype(jnp.bfloat16)


def unpack(geo, slot, received):
    head_rows = 4 * geo.main
    tail_block = geo.chunks * geo.main // geo.tail
    out = jax.ShapeDtypeStruct((geo.slots, geo.features), jnp.bfloat16)
    return pl.pallas_call(
        functools.partial(unpack_kernel, geo),
        grid=(geo.heads,),
        in_specs=[
            pl.BlockSpec(memory_space=pltpu.SMEM),
            pl.BlockSpec((geo.peers, head_rows, LANES), lambda t: (0, t, 0)),
            pl.BlockSpec((geo.peers, geo.tail, LANES), lambda t: (0, tail_block, 0)),
        ],
        out_specs=[pl.BlockSpec((geo.slots, HD), lambda t: (0, t))] * 2,
        out_shape=[out, out],
        scratch_shapes=[
            pltpu.VMEM((geo.joins, geo.window, geo.join * geo.main + geo.peers), jnp.bfloat16),
            pltpu.VMEM((geo.chunks * geo.peers, LANES), jnp.bfloat16),
        ],
        compiler_params=pltpu.CompilerParams(vmem_limit_bytes=VMEM_LIMIT),
        cost_estimate=pl.CostEstimate(
            flops=4 * geo.joins * geo.window * 256 * geo.features,
            bytes_accessed=4 * received.size,
            transcendentals=0,
        ),
    )(slot, received, received)


def merge(one, two):
    half = HD + LANES // 2
    peak_one, peak_two = one[..., HD : HD + 1], two[..., HD : HD + 1]
    peak = jnp.maximum(peak_one, peak_two)
    rescale_one, rescale_two = jnp.exp(peak_one - peak), jnp.exp(peak_two - peak)
    mixed = one * rescale_one + two * rescale_two
    lane = lax.broadcasted_iota(jnp.int32, one.shape, len(one.shape) - 1)
    return jnp.where((lane >= HD) & (lane < half), peak, mixed)


def on_device(
    cache_keys, cache_values, keep_flags, drop_weight, req_blocks, queries, new_keys, new_values,
    out_weight,
):
    peers = lax.axis_size("seq")
    me = lax.axis_index("seq")
    row_count, features = cache_keys.shape
    block_count = row_count // BLOCK
    geo = Geometry(peers, block_count, features)
    req_count = queries.shape[0]
    keep = keep_flags.reshape(block_count, BLOCK)
    weight = drop_weight.reshape(block_count, BLOCK)

    kept_count = jnp.sum(keep, axis=1)
    kept_all = lax.all_to_all(
        jnp.broadcast_to(kept_count[None, :], (peers, block_count)),
        "seq", split_axis=0, concat_axis=0, tiled=True,
    )

    request_ends = jnp.cumsum(req_blocks)
    first = (request_ends - req_blocks - me * block_count)[:, None]
    last = (request_ends - me * block_count)[:, None]
    packed, part = pack(geo, keep, weight, first, last, queries, cache_keys, cache_values)

    counts = jnp.sum(kept_all, axis=1) + block_count
    starts = jnp.cumsum(counts) - counts
    my_start = lax.dynamic_slice(starts, (me,), (1,)) % peers
    sent = turn(geo, my_start, packed)
    received = lax.all_to_all(sent, "seq", split_axis=0, concat_axis=0, tiled=True)
    slot = (starts + (me - starts) % peers) // peers
    packed_keys, packed_values = unpack(geo, slot, received)

    sizes = kept_all.reshape(-1) + 1
    ends = jnp.cumsum(sizes)
    rank = jnp.arange(geo.slots, dtype=jnp.int32) * peers + me
    block = jnp.sum((rank[:, None] >= ends[None, :]).astype(jnp.int32), axis=1)
    folds = rank[:, None] == (ends - 1)[None, :]
    block_bias = jnp.log((BLOCK + 1 - sizes).astype(jnp.float32))
    packed_bias = jnp.sum(jnp.where(folds, block_bias[None, :], 0.0), axis=1).astype(jnp.bfloat16)
    owner = jnp.sum((block[:, None] >= request_ends[None, :]).astype(jnp.int32), axis=1)
    packed_request = jnp.where(rank < ends[-1], owner, -1)

    distance = 1
    while distance < peers:
        pairs = [(i, i ^ distance) for i in range(peers)]
        part = merge(part, lax.ppermute(part, "seq", pairs))
        distance *= 2
    heads = geo.heads
    peak_score, softmax_total = part[..., HD], part[..., HD + LANES // 2]
    weighted = part[..., :HD]
    score_scale = 1.0 / jnp.sqrt(jnp.float32(HD))
    query_heads = queries.reshape(req_count, heads, HD)
    own_score = (
        jnp.einsum(
            "rhd,rhd->hr",
            query_heads,
            new_keys.reshape(req_count, heads, HD),
            preferred_element_type=jnp.float32,
        )
        * score_scale
    )
    final_peak = jnp.maximum(peak_score, own_score)
    rescale_old = jnp.exp(peak_score - final_peak)
    own_prob = jnp.exp(own_score - final_peak)
    new_value_heads = jnp.transpose(new_values.reshape(req_count, heads, HD), (1, 0, 2)).astype(
        jnp.float32
    )
    softmax_total = softmax_total * rescale_old + own_prob
    weighted = weighted * rescale_old[:, :, None] + own_prob[:, :, None] * new_value_heads
    attention_heads = weighted / softmax_total[:, :, None]
    attention = (
        jnp.transpose(attention_heads, (1, 0, 2))
        .reshape(req_count, heads * HD)
        .astype(jnp.bfloat16)
    )
    partial_output = jnp.dot(attention, out_weight, preferred_element_type=jnp.float32)
    layer_output = lax.psum_scatter(partial_output, "tp", scatter_dimension=0, tiled=True).astype(
        jnp.bfloat16
    )
    return (packed_keys, packed_values, packed_bias, packed_request, layer_output)


def solution(mesh):
    in_specs = (
        P("seq", "tp"),
        P("seq", "tp"),
        P("seq"),
        P("seq"),
        P(),
        P(None, "tp"),
        P(None, "tp"),
        P(None, "tp"),
        P("tp", "seq"),
    )
    out_specs = (P("seq", "tp"), P("seq", "tp"), P("seq"), P("seq"), P("tp", "seq"))
    return jax.shard_map(
        on_device, mesh=mesh, in_specs=in_specs, out_specs=out_specs, check_vma=False
    )
```

```python
import functools

import jax
import jax.numpy as jnp
from jax import lax
from jax.experimental import pallas as pl
from jax.experimental.pallas import tpu as pltpu
from jax.sharding import PartitionSpec as P

HD = 256
BLOCK = 128
LANES = 128
SUB = 16
LEAST_KEPT = BLOCK // 4
MOST_KEPT = BLOCK // 2
LOW = -1e30
VMEM_LIMIT = 56 * 1024 * 1024


class Geometry:
    def __init__(self, peers, blocks, features):
        self.peers = peers
        self.blocks = blocks
        self.features = features
        self.heads = features // HD
        self.slots = blocks * (MOST_KEPT + 1)
        self.peer_rows = -(-self.slots // peers)
        self.groups = self.peer_rows // SUB
        self.main = self.groups * SUB
        self.chunks = 2 * features // LANES
        self.tail = -(-self.chunks // SUB) * SUB
        self.slab = self.chunks * self.main + self.tail
        self.group_rows = SUB * peers
        assert self.peer_rows == self.main + 1
        self.join = min(peers, max(1, 256 // self.main))
        self.joins = peers // self.join
        window = self.join * self.peer_rows + SUB - 1
        self.window = min(-(-window // SUB) * SUB, self.slots)
        assert self.slots % SUB == 0 and peers % self.join == 0

    def block_range(self, first, last):
        low = max(0, -(-(first - MOST_KEPT) // (MOST_KEPT + 1)))
        high = min(self.blocks - 1, last // (LEAST_KEPT + 1))
        return low, high + 1


def iota(shape, axis):
    return lax.broadcasted_iota(jnp.int32, shape, axis)


def dot(a, b, contract=((1,), (0,))):
    return lax.dot_general(a, b, (contract, ((), ())), preferred_element_type=jnp.float32)


def pack_kernel(
    geo, keep_ref, weight_ref, first_ref, last_ref, query_ref, key_ref, value_ref,
    packed_ref, part_ref, pick_ref, scale_ref, fold_ref, left_ref,
):
    step = pl.program_id(0)
    blocks, peers = geo.blocks, geo.peers
    ranges = [
        geo.block_range(g * geo.group_rows, (g + 1) * geo.group_rows - 1) for g in range(geo.groups)
    ]
    places = []
    place = 0
    for low, high in ranges:
        places.append(place)
        place += (high - low) * BLOCK
    tail_low, tail_high = geo.block_range(geo.main * peers, geo.slots - 1)
    tail_place = place

    keep = keep_ref[...].astype(jnp.float32)
    kept = jnp.sum(keep, axis=1, keepdims=True)
    dropped = weight_ref[...].astype(jnp.float32) * (1.0 - keep)
    inverse = 1.0 / jnp.sum(dropped, axis=1, keepdims=True)

    @pl.when(step == 0)
    def _():
        earlier = (iota((BLOCK, BLOCK), 0) < iota((BLOCK, BLOCK), 1)).astype(jnp.bfloat16)
        within = dot(keep.astype(jnp.bfloat16), earlier)
        before = (iota((blocks, blocks), 1) < iota((blocks, blocks), 0)).astype(jnp.bfloat16)
        sizes = jnp.broadcast_to(kept + 1.0, (blocks, BLOCK)).astype(jnp.bfloat16)
        base = dot(before, sizes)
        entry = jnp.where(keep > 0.0, base + within, -1.0).astype(jnp.int32)
        fold_entry = (base + kept).astype(jnp.int32)

        def select(index, low, high, rows, place):
            scale = jnp.ones((rows, BLOCK), jnp.float32)
            for b in range(low, high):
                folds = index == fold_entry[b : b + 1, :]
                one = jnp.where(index == entry[b : b + 1, :], 1.0, 0.0)
                picked = jnp.where(folds, dropped[b : b + 1, :], one)
                at = place + (b - low) * BLOCK
                pick_ref[0:rows, at : at + BLOCK] = picked.astype(jnp.bfloat16)
                scale = jnp.where(folds, inverse[b : b + 1, :], scale)
            return scale

        rows = geo.group_rows
        row, col = iota((rows, BLOCK), 0), 0
        for g in range(geo.groups):
            index = (g * SUB + row % SUB) * peers + row // SUB
            scale_ref[g, :, :] = select(index, *ranges[g], rows, places[g])
        index = geo.main * peers + iota((peers, BLOCK), 0)
        scale_ref[geo.groups, 0:peers, :] = select(index, tail_low, tail_high, peers, tail_place)
        for b in range(blocks):
            mine = iota((blocks, BLOCK), 0) == b
            fold_ref[:, b * BLOCK : (b + 1) * BLOCK] = jnp.where(
                mine, dropped[b : b + 1, :], 0.0
            ).astype(jnp.bfloat16)

    for part, source in enumerate((key_ref, value_ref)):
        for g in range(geo.groups):
            low, high = ranges[g]
            rows = dot(
                pick_ref[:, places[g] : places[g] + (high - low) * BLOCK],
                source[low * BLOCK : high * BLOCK, :],
            )
            for half in range(HD // LANES):
                chunk = rows[:, half * LANES : (half + 1) * LANES] * scale_ref[g]
                chunk = chunk.astype(jnp.bfloat16).reshape(peers, SUB, LANES)
                at = pl.multiple_of(
                    (step * 4 + part * 2 + half) * geo.main + g * SUB, SUB
                )
                packed_ref[:, pl.ds(at, SUB), :] = chunk
        tail = dot(
            pick_ref[0:peers, tail_place : tail_place + (tail_high - tail_low) * BLOCK],
            source[tail_low * BLOCK : tail_high * BLOCK, :],
        )
        for half in range(HD // LANES):
            chunk = tail[:, half * LANES : (half + 1) * LANES] * scale_ref[geo.groups, 0:peers, :]
            at = pl.multiple_of((step * 4 + part * 2 + half) * peers, SUB)
            left_ref[pl.ds(at, peers), :] = chunk.astype(jnp.bfloat16)

    @pl.when(step == geo.heads - 1)
    def _():
        shape = (peers * geo.tail, geo.chunks * peers)
        row, col = iota(shape, 0), iota(shape, 1)
        wanted = row % geo.tail * peers + row // geo.tail
        turn = jnp.where(wanted == col, 1.0, 0.0).astype(jnp.bfloat16)
        tails = dot(turn, left_ref[...]).astype(jnp.bfloat16).reshape(peers, geo.tail, LANES)
        packed_ref[:, geo.chunks * geo.main :, :] = tails

    query = query_ref[...]
    first, last = first_ref[...], last_ref[...]
    requests = query.shape[0]
    score_scale = HD**-0.5
    folded_keys = (dot(fold_ref[...], key_ref[...]) * inverse).astype(jnp.bfloat16)
    folded_values = (dot(fold_ref[...], value_ref[...]) * inverse).astype(jnp.bfloat16)
    ones = jnp.ones((8, BLOCK), jnp.bfloat16)
    kept_lanes = dot(ones, keep.astype(jnp.bfloat16), ((1,), (1,)))[0:1, :]
    bias = jnp.log(BLOCK - kept_lanes).astype(jnp.bfloat16).astype(jnp.float32)
    fold_scores = dot(query, folded_keys, ((1,), (1,))) * score_scale + bias
    block = iota((requests, blocks), 1)
    fold_member = (block >= first) & (block < last)
    fold_scores = jnp.where(fold_member, fold_scores, LOW)
    scores = dot(query, key_ref[...], ((1,), (1,))) * score_scale
    lane_block = iota((requests, blocks * BLOCK), 1) // BLOCK
    kept_rows = jnp.concatenate(
        [jnp.broadcast_to(keep[b : b + 1, :], (requests, BLOCK)) for b in range(blocks)], axis=1
    )
    member = (lane_block >= first) & (lane_block < last) & (kept_rows > 0.0)
    scores = jnp.where(member, scores, LOW)
    peak = jnp.maximum(
        jnp.max(scores, axis=1, keepdims=True), jnp.max(fold_scores, axis=1, keepdims=True)
    )
    probs = jnp.where(member, jnp.exp(scores - peak), 0.0)
    fold_probs = jnp.where(fold_member, jnp.exp(fold_scores - peak), 0.0)
    total = jnp.sum(probs, axis=1, keepdims=True) + jnp.sum(fold_probs, axis=1, keepdims=True)
    mixed = dot(probs.astype(jnp.bfloat16), value_ref[...]) + dot(
        fold_probs.astype(jnp.bfloat16), folded_values
    )
    part_ref[0, :, 0:HD] = mixed
    part_ref[0, :, HD:] = jnp.where(iota((requests, LANES), 1) < LANES // 2, peak, total)


def pack(geo, keep, weight, first, last, queries, cache_keys, cache_values):
    rows = cache_keys.shape[0]
    requests = queries.shape[0]
    width = 0
    for g in range(geo.groups):
        low, high = geo.block_range(g * geo.group_rows, (g + 1) * geo.group_rows - 1)
        width += (high - low) * BLOCK
    low, high = geo.block_range(geo.main * geo.peers, geo.slots - 1)
    width += (high - low) * BLOCK
    whole = lambda *shape: pl.BlockSpec(shape, lambda t: (0,) * len(shape))
    return pl.pallas_call(
        functools.partial(pack_kernel, geo),
        grid=(geo.heads,),
        in_specs=[
            whole(geo.blocks, BLOCK),
            whole(geo.blocks, BLOCK),
            whole(requests, 1),
            whole(requests, 1),
            pl.BlockSpec((requests, HD), lambda t: (0, t)),
            pl.BlockSpec((rows, HD), lambda t: (0, t)),
            pl.BlockSpec((rows, HD), lambda t: (0, t)),
        ],
        out_specs=[
            whole(geo.peers, geo.slab, LANES),
            pl.BlockSpec((1, requests, HD + LANES), lambda t: (t, 0, 0)),
        ],
        out_shape=[
            jax.ShapeDtypeStruct((geo.peers, geo.slab, LANES), jnp.bfloat16),
            jax.ShapeDtypeStruct((geo.heads, requests, HD + LANES), jnp.float32),
        ],
        scratch_shapes=[
            pltpu.VMEM((geo.group_rows, width), jnp.bfloat16),
            pltpu.VMEM((geo.groups + 1, geo.group_rows, BLOCK), jnp.float32),
            pltpu.VMEM((geo.blocks, rows), jnp.bfloat16),
            pltpu.VMEM((geo.chunks * geo.peers, LANES), jnp.bfloat16),
        ],
        compiler_params=pltpu.CompilerParams(vmem_limit_bytes=VMEM_LIMIT),
        cost_estimate=pl.CostEstimate(
            flops=2 * geo.group_rows * width * 2 * geo.features,
            bytes_accessed=3 * rows * geo.features * 2,
            transcendentals=0,
        ),
    )(keep, weight, first, last, queries, cache_keys, cache_values)


def turn_kernel(geo, start_ref, packed_ref, sent_ref, sems):
    start = start_ref[0]
    copies = []
    for d in range(geo.peers):
        group = lax.rem(d + geo.peers - start, geo.peers)
        copies.append(pltpu.make_async_copy(packed_ref.at[group], sent_ref.at[d], sems.at[d]))
    for copy in copies:
        copy.start()
    for copy in copies:
        copy.wait()


def turn(geo, start, packed):
    return pl.pallas_call(
        functools.partial(turn_kernel, geo),
        in_specs=[pl.BlockSpec(memory_space=pltpu.SMEM), pl.BlockSpec(memory_space=pltpu.VMEM)],
        out_specs=pl.BlockSpec(memory_space=pl.ANY),
        out_shape=jax.ShapeDtypeStruct(packed.shape, packed.dtype),
        scratch_shapes=[pltpu.SemaphoreType.DMA((geo.peers,))],
        compiler_params=pltpu.CompilerParams(vmem_limit_bytes=VMEM_LIMIT),
        cost_estimate=pl.CostEstimate(flops=0, bytes_accessed=2 * packed.size * 2, transcendentals=0),
    )(start, packed)


def unpack_kernel(geo, slot_ref, slab_ref, tail_ref, keys_ref, values_ref, pick_ref, tails_ref):
    step = pl.program_id(0)
    peers, main = geo.peers, geo.main
    width = geo.join * main
    lows = []
    for q in range(geo.joins):
        low = jnp.minimum(slot_ref[q * geo.join] // SUB * SUB, geo.slots - geo.window)
        lows.append(pl.multiple_of(low, SUB))

    @pl.when(step == 0)
    def _():
        for q in range(geo.joins):
            lane = iota((1, width), 1)
            target = lane % main
            last = iota((1, peers), 1) * 0 - 1
            for j in range(geo.join):
                at = slot_ref[q * geo.join + j] - lows[q]
                target = target + jnp.where(lane // main == j, at, 0)
                last = jnp.where(iota((1, peers), 1) == q * geo.join + j, at + main, last)
            picked = jnp.where(iota((geo.window, width), 0) == target, 1.0, 0.0)
            pick_ref[q, :, 0:width] = picked.astype(jnp.bfloat16)
            picked = jnp.where(iota((geo.window, peers), 0) == last, 1.0, 0.0)
            pick_ref[q, :, width : width + peers] = picked.astype(jnp.bfloat16)
        shape = (geo.chunks * peers, peers * geo.tail)
        row, col = iota(shape, 0), iota(shape, 1)
        wanted = row % peers * geo.tail + row // peers
        back = jnp.where(wanted == col, 1.0, 0.0).astype(jnp.bfloat16)
        tails = tail_ref[...].reshape(peers * geo.tail, LANES)
        tails_ref[...] = dot(back, tails).astype(jnp.bfloat16)

    for part, out_ref in enumerate((keys_ref, values_ref)):
        out_ref[...] = jnp.zeros_like(out_ref)
        halves = [part * 2 + half for half in range(HD // LANES)]
        tails = jnp.concatenate(
            [tails_ref[pl.ds(pl.multiple_of((step * 4 + c) * peers, SUB), peers), :] for c in halves],
            axis=1,
        )
        for q in range(geo.joins):
            rows = jnp.concatenate(
                [
                    slab_ref[
                        q * geo.join : (q + 1) * geo.join, c * main : (c + 1) * main, :
                    ].reshape(width, LANES)
                    for c in halves
                ],
                axis=1,
            )
            placed = dot(pick_ref[q, :, 0:width], rows)
            placed = placed + dot(pick_ref[q, :, width : width + peers], tails)
            out_ref[pl.ds(lows[q], geo.window), :] += placed.astype(jnp.bfloat16)


def unpack(geo, slot, received):
    head_rows = 4 * geo.main
    tail_block = geo.chunks * geo.main // geo.tail
    out = jax.ShapeDtypeStruct((geo.slots, geo.features), jnp.bfloat16)
    return pl.pallas_call(
        functools.partial(unpack_kernel, geo),
        grid=(geo.heads,),
        in_specs=[
            pl.BlockSpec(memory_space=pltpu.SMEM),
            pl.BlockSpec((geo.peers, head_rows, LANES), lambda t: (0, t, 0)),
            pl.BlockSpec((geo.peers, geo.tail, LANES), lambda t: (0, tail_block, 0)),
        ],
        out_specs=[pl.BlockSpec((geo.slots, HD), lambda t: (0, t))] * 2,
        out_shape=[out, out],
        scratch_shapes=[
            pltpu.VMEM((geo.joins, geo.window, geo.join * geo.main + geo.peers), jnp.bfloat16),
            pltpu.VMEM((geo.chunks * geo.peers, LANES), jnp.bfloat16),
        ],
        compiler_params=pltpu.CompilerParams(vmem_limit_bytes=VMEM_LIMIT),
        cost_estimate=pl.CostEstimate(
            flops=4 * geo.joins * geo.window * 256 * geo.features,
            bytes_accessed=4 * received.size,
            transcendentals=0,
        ),
    )(slot, received, received)


def merge(one, two):
    half = HD + LANES // 2
    peak_one, peak_two = one[..., HD : HD + 1], two[..., HD : HD + 1]
    peak = jnp.maximum(peak_one, peak_two)
    rescale_one, rescale_two = jnp.exp(peak_one - peak), jnp.exp(peak_two - peak)
    mixed = one * rescale_one + two * rescale_two
    lane = lax.broadcasted_iota(jnp.int32, one.shape, len(one.shape) - 1)
    return jnp.where((lane >= HD) & (lane < half), peak, mixed)


def on_device(
    cache_keys, cache_values, keep_flags, drop_weight, req_blocks, queries, new_keys, new_values,
    out_weight,
):
    peers = lax.axis_size("seq")
    me = lax.axis_index("seq")
    row_count, features = cache_keys.shape
    block_count = row_count // BLOCK
    geo = Geometry(peers, block_count, features)
    req_count = queries.shape[0]
    keep = keep_flags.reshape(block_count, BLOCK)
    weight = drop_weight.reshape(block_count, BLOCK)

    kept_count = jnp.sum(keep, axis=1)
    kept_all = lax.all_to_all(
        jnp.broadcast_to(kept_count[None, :], (peers, block_count)),
        "seq", split_axis=0, concat_axis=0, tiled=True,
    )

    request_ends = jnp.cumsum(req_blocks)
    first = (request_ends - req_blocks - me * block_count)[:, None]
    last = (request_ends - me * block_count)[:, None]
    packed, part = pack(geo, keep, weight, first, last, queries, cache_keys, cache_values)

    counts = jnp.sum(kept_all, axis=1) + block_count
    starts = jnp.cumsum(counts) - counts
    my_start = lax.dynamic_slice(starts, (me,), (1,)) % peers
    sent = turn(geo, my_start, packed)
    received = lax.all_to_all(sent, "seq", split_axis=0, concat_axis=0, tiled=True)
    slot = (starts + (me - starts) % peers) // peers
    packed_keys, packed_values = unpack(geo, slot, received)

    sizes = kept_all.reshape(-1) + 1
    ends = jnp.cumsum(sizes)
    rank = jnp.arange(geo.slots, dtype=jnp.int32) * peers + me
    block = jnp.sum((rank[:, None] >= ends[None, :]).astype(jnp.int32), axis=1)
    folds = rank[:, None] == (ends - 1)[None, :]
    block_bias = jnp.log((BLOCK + 1 - sizes).astype(jnp.float32))
    packed_bias = jnp.sum(jnp.where(folds, block_bias[None, :], 0.0), axis=1).astype(jnp.bfloat16)
    owner = jnp.sum((block[:, None] >= request_ends[None, :]).astype(jnp.int32), axis=1)
    packed_request = jnp.where(rank < ends[-1], owner, -1)

    distance = 1
    while distance < peers:
        pairs = [(i, i ^ distance) for i in range(peers)]
        part = merge(part, lax.ppermute(part, "seq", pairs))
        distance *= 2
    heads = geo.heads
    peak_score, softmax_total = part[..., HD], part[..., HD + LANES // 2]
    weighted = part[..., :HD]
    score_scale = 1.0 / jnp.sqrt(jnp.float32(HD))
    query_heads = queries.reshape(req_count, heads, HD)
    own_score = (
        jnp.einsum(
            "rhd,rhd->hr",
            query_heads,
            new_keys.reshape(req_count, heads, HD),
            preferred_element_type=jnp.float32,
        )
        * score_scale
    )
    final_peak = jnp.maximum(peak_score, own_score)
    rescale_old = jnp.exp(peak_score - final_peak)
    own_prob = jnp.exp(own_score - final_peak)
    new_value_heads = jnp.transpose(new_values.reshape(req_count, heads, HD), (1, 0, 2)).astype(
        jnp.float32
    )
    softmax_total = softmax_total * rescale_old + own_prob
    weighted = weighted * rescale_old[:, :, None] + own_prob[:, :, None] * new_value_heads
    attention_heads = weighted / softmax_total[:, :, None]
    attention = (
        jnp.transpose(attention_heads, (1, 0, 2))
        .reshape(req_count, heads * HD)
        .astype(jnp.bfloat16)
    )
    partial_output = jnp.dot(attention, out_weight, preferred_element_type=jnp.float32)
    layer_output = lax.psum_scatter(partial_output, "tp", scatter_dimension=0, tiled=True).astype(
        jnp.bfloat16
    )
    return (packed_keys, packed_values, packed_bias, packed_request, layer_output)


def solution(mesh):
    in_specs = (
        P("seq", "tp"),
        P("seq", "tp"),
        P("seq"),
        P("seq"),
        P(),
        P(None, "tp"),
        P(None, "tp"),
        P(None, "tp"),
        P("tp", "seq"),
    )
    out_specs = (P("seq", "tp"), P("seq", "tp"), P("seq"), P("seq"), P("tp", "seq"))
    return jax.shard_map(
        on_device, mesh=mesh, in_specs=in_specs, out_specs=out_specs, check_vma=False
    )
```

```python
import functools

import jax
import jax.numpy as jnp
from jax import lax
from jax.experimental import pallas as pl
from jax.experimental.pallas import tpu as pltpu
from jax.sharding import PartitionSpec as P

HD = 256
BLOCK = 128
LANES = 128
SUB = 16
LEAST_KEPT = BLOCK // 4
MOST_KEPT = BLOCK // 2
LOW = -1e30
VMEM_LIMIT = 56 * 1024 * 1024


class Geometry:
    def __init__(self, peers, blocks, features):
        self.peers = peers
        self.blocks = blocks
        self.features = features
        self.heads = features // HD
        self.slots = blocks * (MOST_KEPT + 1)
        self.peer_rows = -(-self.slots // peers)
        self.groups = self.peer_rows // SUB
        self.main = self.groups * SUB
        self.chunks = 2 * features // LANES
        self.tail = -(-self.chunks // SUB) * SUB
        self.share = self.chunks // 2 * self.main
        self.group_rows = SUB * peers
        assert self.peer_rows == self.main + 1
        assert self.block_range(self.main * peers, self.slots - 1) == (blocks - 1, blocks)
        self.join = min(peers, max(1, 256 // self.main))
        self.joins = peers // self.join
        window = self.join * self.peer_rows + SUB - 1
        self.window = min(-(-window // SUB) * SUB, self.slots)
        assert self.slots % SUB == 0 and peers % self.join == 0

    def block_range(self, first, last):
        low = max(0, -(-(first - MOST_KEPT) // (MOST_KEPT + 1)))
        high = min(self.blocks - 1, last // (LEAST_KEPT + 1))
        return low, high + 1

    def ranges(self):
        rows = self.group_rows
        return [self.block_range(g * rows, (g + 1) * rows - 1) for g in range(self.groups)]

    def places(self):
        places = [0]
        for low, high in self.ranges():
            places.append(places[-1] + (high - low) * BLOCK)
        return places


def iota(shape, axis):
    return lax.broadcasted_iota(jnp.int32, shape, axis)


def dot(a, b, contract=((1,), (0,))):
    return lax.dot_general(a, b, (contract, ((), ())), preferred_element_type=jnp.float32)


def pack_kernel(geo, tails, keep_ref, weight_ref, cache_ref, *refs):
    step = pl.program_id(0)
    blocks, peers = geo.blocks, geo.peers
    if tails:
        end_refs, (main_ref, tail_ref, pick_ref, scale_ref) = refs[:2], refs[2:]
    else:
        main_ref, pick_ref, scale_ref = refs
    ranges = geo.ranges()
    places = geo.places()

    def flags():
        keep = keep_ref[...].reshape(blocks, BLOCK).astype(jnp.float32)
        weight = weight_ref[...].reshape(blocks, BLOCK).astype(jnp.float32)
        return keep, weight * (1.0 - keep)

    @pl.when(step == 0)
    def _():
        keep, dropped = flags()
        kept = jnp.sum(keep, axis=1, keepdims=True)
        inverse = 1.0 / jnp.sum(dropped, axis=1, keepdims=True)
        earlier = (iota((BLOCK, BLOCK), 0) < iota((BLOCK, BLOCK), 1)).astype(jnp.bfloat16)
        within = dot(keep.astype(jnp.bfloat16), earlier)
        before = (iota((blocks, blocks), 1) < iota((blocks, blocks), 0)).astype(jnp.bfloat16)
        sizes = jnp.broadcast_to(kept + 1.0, (blocks, BLOCK)).astype(jnp.bfloat16)
        base = dot(before, sizes)
        entry = jnp.where(keep > 0.0, base + within, -1.0).astype(jnp.int32)
        fold_entry = (base + kept).astype(jnp.int32)

        def select(index, low, high):
            scale = jnp.ones(index.shape, jnp.float32)
            picks = []
            for b in range(low, high):
                folds = index == fold_entry[b : b + 1, :]
                one = jnp.where(index == entry[b : b + 1, :], 1.0, 0.0)
                picked = jnp.where(folds, dropped[b : b + 1, :], one)
                picks.append(picked.astype(jnp.bfloat16))
                scale = jnp.where(folds, inverse[b : b + 1, :], scale)
            return picks, scale

        row = iota((geo.group_rows, BLOCK), 0)
        for g in range(geo.groups):
            index = (g * SUB + row % SUB) * peers + row // SUB
            picks, scale_ref[g, :, :] = select(index, *ranges[g])
            for i, picked in enumerate(picks):
                at = places[g] + i * BLOCK
                pick_ref[:, at : at + BLOCK] = picked
        if tails:
            index = geo.main * peers + iota((peers, BLOCK), 0)
            (picked,), scale = select(index, blocks - 1, blocks)
            left = []
            for end_ref in end_refs:
                rows = dot(picked, end_ref[...])
                for c in range(geo.chunks // 2):
                    left.append((rows[:, c * LANES : (c + 1) * LANES] * scale).astype(jnp.bfloat16))
            shape = (peers * geo.tail, geo.chunks * peers)
            row, col = iota(shape, 0), iota(shape, 1)
            wanted = row % geo.tail * peers + row // geo.tail
            turn = jnp.where(wanted == col, 1.0, 0.0).astype(jnp.bfloat16)
            rows = dot(turn, jnp.concatenate(left, axis=0)).astype(jnp.bfloat16)
            tail_ref[...] = rows.reshape(peers, geo.tail, LANES)

    for g in range(geo.groups):
        low, high = ranges[g]
        rows = dot(
            pick_ref[:, places[g] : places[g] + (high - low) * BLOCK],
            cache_ref[low * BLOCK : high * BLOCK, :],
        )
        for half in range(HD // LANES):
            chunk = rows[:, half * LANES : (half + 1) * LANES] * scale_ref[g]
            chunk = chunk.astype(jnp.bfloat16).reshape(peers, SUB, LANES)
            at = half * geo.main + g * SUB
            main_ref[:, at : at + SUB, :] = chunk


def attend_kernel(
    geo, keep_ref, weight_ref, first_ref, last_ref, query_ref, key_ref, value_ref,
    part_ref, fold_ref,
):
    step = pl.program_id(0)
    blocks = geo.blocks
    keep = keep_ref[...].reshape(blocks, BLOCK).astype(jnp.float32)
    weight = weight_ref[...].reshape(blocks, BLOCK).astype(jnp.float32)
    dropped = weight * (1.0 - keep)
    inverse = 1.0 / jnp.sum(dropped, axis=1, keepdims=True)

    @pl.when(step == 0)
    def _():
        for b in range(blocks):
            mine = iota((blocks, BLOCK), 0) == b
            fold_ref[:, b * BLOCK : (b + 1) * BLOCK] = jnp.where(
                mine, dropped[b : b + 1, :], 0.0
            ).astype(jnp.bfloat16)

    query = query_ref[...]
    first, last = first_ref[...], last_ref[...]
    requests = query.shape[0]
    score_scale = HD**-0.5
    folded_keys = (dot(fold_ref[...], key_ref[...]) * inverse).astype(jnp.bfloat16)
    folded_values = (dot(fold_ref[...], value_ref[...]) * inverse).astype(jnp.bfloat16)
    ones = jnp.ones((8, BLOCK), jnp.bfloat16)
    kept_lanes = dot(ones, keep.astype(jnp.bfloat16), ((1,), (1,)))[0:1, :]
    bias = jnp.log(BLOCK - kept_lanes).astype(jnp.bfloat16).astype(jnp.float32)
    fold_scores = dot(query, folded_keys, ((1,), (1,))) * score_scale + bias
    block = iota((requests, blocks), 1)
    fold_member = (block >= first) & (block < last)
    fold_scores = jnp.where(fold_member, fold_scores, LOW)
    scores = dot(query, key_ref[...], ((1,), (1,))) * score_scale
    lane_block = iota((requests, blocks * BLOCK), 1) // BLOCK
    kept_rows = jnp.concatenate(
        [jnp.broadcast_to(keep[b : b + 1, :], (requests, BLOCK)) for b in range(blocks)], axis=1
    )
    member = (lane_block >= first) & (lane_block < last) & (kept_rows > 0.0)
    scores = jnp.where(member, scores, LOW)
    peak = jnp.maximum(
        jnp.max(scores, axis=1, keepdims=True), jnp.max(fold_scores, axis=1, keepdims=True)
    )
    probs = jnp.where(member, jnp.exp(scores - peak), 0.0)
    fold_probs = jnp.where(fold_member, jnp.exp(fold_scores - peak), 0.0)
    total = jnp.sum(probs, axis=1, keepdims=True) + jnp.sum(fold_probs, axis=1, keepdims=True)
    mixed = dot(probs.astype(jnp.bfloat16), value_ref[...]) + dot(
        fold_probs.astype(jnp.bfloat16), folded_values
    )
    part_ref[0, :, 0:HD] = mixed
    part_ref[0, :, HD:] = jnp.where(iota((requests, LANES), 1) < LANES // 2, peak, total)


def whole(*shape):
    return pl.BlockSpec(shape, lambda t: (0,) * len(shape))


def pack(geo, keep, weight, cache, ends=()):
    rows = cache.shape[0]
    width = geo.places()[-1]
    end_block = geo.blocks - 1
    out_specs = [pl.BlockSpec((geo.peers, 2 * geo.main, LANES), lambda t: (0, t, 0))]
    out_shape = [jax.ShapeDtypeStruct((geo.peers, geo.share, LANES), jnp.bfloat16)]
    if ends:
        out_specs.append(whole(geo.peers, geo.tail, LANES))
        out_shape.append(jax.ShapeDtypeStruct((geo.peers, geo.tail, LANES), jnp.bfloat16))
    return pl.pallas_call(
        functools.partial(pack_kernel, geo, bool(ends)),
        grid=(geo.heads,),
        in_specs=[whole(rows), whole(rows), pl.BlockSpec((rows, HD), lambda t: (0, t))]
        + [pl.BlockSpec((BLOCK, geo.features), lambda t: (end_block, 0))] * len(ends),
        out_specs=out_specs,
        out_shape=out_shape,
        scratch_shapes=[
            pltpu.VMEM((geo.group_rows, width), jnp.bfloat16),
            pltpu.VMEM((geo.groups, geo.group_rows, BLOCK), jnp.float32),
        ],
        compiler_params=pltpu.CompilerParams(vmem_limit_bytes=VMEM_LIMIT),
        cost_estimate=pl.CostEstimate(
            flops=2 * geo.group_rows * width * geo.features,
            bytes_accessed=3 * rows * geo.features,
            transcendentals=0,
        ),
    )(keep, weight, cache, *ends)


def attend(geo, keep, weight, first, last, queries, cache_keys, cache_values):
    rows = cache_keys.shape[0]
    requests = queries.shape[0]
    return pl.pallas_call(
        functools.partial(attend_kernel, geo),
        grid=(geo.heads,),
        in_specs=[
            whole(rows),
            whole(rows),
            whole(requests, 1),
            whole(requests, 1),
            pl.BlockSpec((requests, HD), lambda t: (0, t)),
            pl.BlockSpec((rows, HD), lambda t: (0, t)),
            pl.BlockSpec((rows, HD), lambda t: (0, t)),
        ],
        out_specs=pl.BlockSpec((1, requests, HD + LANES), lambda t: (t, 0, 0)),
        out_shape=jax.ShapeDtypeStruct((geo.heads, requests, HD + LANES), jnp.float32),
        scratch_shapes=[pltpu.VMEM((geo.blocks, rows), jnp.bfloat16)],
        compiler_params=pltpu.CompilerParams(vmem_limit_bytes=VMEM_LIMIT),
        cost_estimate=pl.CostEstimate(
            flops=8 * rows * requests * geo.features,
            bytes_accessed=2 * rows * geo.features * 2,
            transcendentals=rows * requests * geo.heads,
        ),
    )(keep, weight, first, last, queries, cache_keys, cache_values)


def my_start(kept, me):
    return jnp.sum(jnp.where(iota(kept.shape, 0) < me, kept + 1, 0))


def turn_kernel(geo, kept_ref, *refs):
    main_ref, tail_refs = refs[0], refs[1:-4]
    sent_ref, held_ref, in_sems, out_sems = refs[-4:]
    me = lax.axis_index("seq")
    peers, share = geo.peers, geo.share
    arrivals = []
    for p in range(peers):
        held = held_ref.at[p]
        copies = [pltpu.make_async_copy(main_ref.at[p], held.at[0:share], in_sems.at[0, p])]
        for tail_ref in tail_refs:
            tail = held.at[share : share + geo.tail]
            copies.append(pltpu.make_async_copy(tail_ref.at[p], tail, in_sems.at[1, p]))
        for copy in copies:
            copy.start()
        arrivals.append(copies)
    start = my_start(kept_ref[...], me)
    departures = []
    for p in range(peers):
        device = lax.rem(start + p, peers)
        for copy in arrivals[p]:
            copy.wait()
        departures.append(
            pltpu.make_async_copy(held_ref.at[p], sent_ref.at[device], out_sems.at[p])
        )
        departures[p].start()
    for copy in departures:
        copy.wait()


def turn(geo, kept, main, tail=None):
    tails = [] if tail is None else [tail]
    shape = (geo.peers, geo.share + len(tails) * geo.tail, LANES)
    size = geo.peers * geo.share * LANES
    return pl.pallas_call(
        functools.partial(turn_kernel, geo),
        in_specs=[pl.BlockSpec(memory_space=pltpu.VMEM)]
        + [pl.BlockSpec(memory_space=pl.ANY)] * (1 + len(tails)),
        out_specs=pl.BlockSpec(memory_space=pl.ANY),
        out_shape=jax.ShapeDtypeStruct(shape, jnp.bfloat16),
        scratch_shapes=[
            pltpu.VMEM(shape, jnp.bfloat16),
            pltpu.SemaphoreType.DMA((2, geo.peers)),
            pltpu.SemaphoreType.DMA((geo.peers,)),
        ],
        compiler_params=pltpu.CompilerParams(vmem_limit_bytes=VMEM_LIMIT),
        cost_estimate=pl.CostEstimate(flops=0, bytes_accessed=4 * size, transcendentals=0),
    )(kept, main, *tails)


def unpack_kernel(geo, part, slot_ref, slab_ref, tail_ref, out_ref, pick_ref, tails_ref):
    peers, main = geo.peers, geo.main
    step = pl.program_id(0)
    width = geo.join * main
    halves = HD // LANES
    lows = []
    for q in range(geo.joins):
        low = jnp.minimum(slot_ref[q * geo.join] // SUB * SUB, geo.slots - geo.window)
        lows.append(pl.multiple_of(low, SUB))

    @pl.when(step == 0)
    def _():
        for q in range(geo.joins):
            lane = iota((1, width), 1)
            target = lane % main
            last = jnp.full((1, peers), -1, jnp.int32)
            for j in range(geo.join):
                at = slot_ref[q * geo.join + j] - lows[q]
                target = target + jnp.where(lane // main == j, at, 0)
                last = jnp.where(iota((1, peers), 1) == q * geo.join + j, at + main, last)
            picked = jnp.where(iota((geo.window, width), 0) == target, 1.0, 0.0)
            pick_ref[q, :, 0:width] = picked.astype(jnp.bfloat16)
            picked = jnp.where(iota((geo.window, peers), 0) == last, 1.0, 0.0)
            pick_ref[q, :, width : width + peers] = picked.astype(jnp.bfloat16)
        share = geo.chunks // 2
        shape = (share * peers, peers * geo.tail)
        row, col = iota(shape, 0), iota(shape, 1)
        wanted = row % peers * geo.tail + row // peers + part * share
        back = jnp.where(wanted == col, 1.0, 0.0).astype(jnp.bfloat16)
        tails = tail_ref[...].reshape(peers * geo.tail, LANES)
        tails_ref[...] = dot(back, tails).astype(jnp.bfloat16)

    out_ref[...] = jnp.zeros_like(out_ref)
    tails = jnp.concatenate(
        [
            tails_ref[pl.ds(pl.multiple_of((step * halves + c) * peers, SUB), peers), :]
            for c in range(halves)
        ],
        axis=1,
    )
    for q in range(geo.joins):
        sources = slice(q * geo.join, (q + 1) * geo.join)
        rows = [
            slab_ref[sources, c * main : (c + 1) * main, :].reshape(width, LANES)
            for c in range(halves)
        ]
        placed = dot(pick_ref[q, :, 0:width], jnp.concatenate(rows, axis=1))
        placed = placed + dot(pick_ref[q, :, width : width + peers], tails)
        out_ref[pl.ds(lows[q], geo.window), :] += placed.astype(jnp.bfloat16)


def unpack(geo, part, slot, slabs, tail):
    head_rows = HD // LANES * geo.main
    tail_block = geo.share // geo.tail
    return pl.pallas_call(
        functools.partial(unpack_kernel, geo, part),
        grid=(geo.heads,),
        in_specs=[
            pl.BlockSpec(memory_space=pltpu.SMEM),
            pl.BlockSpec((geo.peers, head_rows, LANES), lambda t: (0, t, 0)),
            pl.BlockSpec((geo.peers, geo.tail, LANES), lambda t: (0, tail_block, 0)),
        ],
        out_specs=pl.BlockSpec((geo.slots, HD), lambda t: (0, t)),
        out_shape=jax.ShapeDtypeStruct((geo.slots, geo.features), jnp.bfloat16),
        scratch_shapes=[
            pltpu.VMEM((geo.joins, geo.window, geo.join * geo.main + geo.peers), jnp.bfloat16),
            pltpu.VMEM((geo.chunks // 2 * geo.peers, LANES), jnp.bfloat16),
        ],
        compiler_params=pltpu.CompilerParams(vmem_limit_bytes=VMEM_LIMIT),
        cost_estimate=pl.CostEstimate(
            flops=2 * geo.joins * geo.window * 256 * geo.features,
            bytes_accessed=4 * geo.peers * geo.share * LANES,
            transcendentals=0,
        ),
    )(slot, slabs, tail)


def merge(one, two):
    half = HD + LANES // 2
    peak_one, peak_two = one[..., HD : HD + 1], two[..., HD : HD + 1]
    peak = jnp.maximum(peak_one, peak_two)
    rescale_one, rescale_two = jnp.exp(peak_one - peak), jnp.exp(peak_two - peak)
    mixed = one * rescale_one + two * rescale_two
    lane = lax.broadcasted_iota(jnp.int32, one.shape, len(one.shape) - 1)
    return jnp.where((lane >= HD) & (lane < half), peak, mixed)


def on_device(
    cache_keys, cache_values, keep_flags, drop_weight, req_blocks, queries, new_keys, new_values,
    out_weight,
):
    peers = lax.axis_size("seq")
    me = lax.axis_index("seq")
    row_count, features = cache_keys.shape
    block_count = row_count // BLOCK
    geo = Geometry(peers, block_count, features)
    req_count = queries.shape[0]
    kept_count = jnp.sum(keep_flags.reshape(block_count, BLOCK), axis=1)
    kept_all = lax.all_to_all(
        jnp.broadcast_to(kept_count[None, :], (peers, block_count)),
        "seq", split_axis=0, concat_axis=0, tiled=True,
    )

    main, tail = pack(geo, keep_flags, drop_weight, cache_keys, (cache_keys, cache_values))
    sent = turn(geo, kept_all, main, tail)
    tied = (sent, keep_flags, drop_weight, kept_all, req_blocks)
    sent, keep_flags, drop_weight, kept_all, req_blocks = lax.optimization_barrier(tied)
    keys = lax.all_to_all(sent, "seq", split_axis=0, concat_axis=0, tiled=True)

    request_ends = jnp.cumsum(req_blocks)
    first = (request_ends - req_blocks - me * block_count)[:, None]
    last = (request_ends - me * block_count)[:, None]
    part = attend(geo, keep_flags, drop_weight, first, last, queries, cache_keys, cache_values)
    (main,) = pack(geo, keep_flags, drop_weight, cache_values)
    sent = turn(geo, kept_all, main)
    distance = 1
    while distance < peers:
        if distance == peers // 2:
            part, sent = lax.optimization_barrier((part, sent))
        pairs = [(i, i ^ distance) for i in range(peers)]
        part = merge(part, lax.ppermute(part, "seq", pairs))
        distance *= 2
    part, sent = lax.optimization_barrier((part, sent))
    values = lax.all_to_all(sent, "seq", split_axis=0, concat_axis=0, tiled=True)

    counts = jnp.sum(kept_all, axis=1) + block_count
    starts = jnp.cumsum(counts) - counts
    slot = (starts + (me - starts) % peers) // peers
    packed_keys = unpack(geo, 0, slot, keys, keys)
    packed_values = unpack(geo, 1, slot, values, keys)

    sizes = kept_all.reshape(-1) + 1
    ends = jnp.cumsum(sizes)
    rank = jnp.arange(geo.slots, dtype=jnp.int32) * peers + me
    block = jnp.sum((rank[:, None] >= ends[None, :]).astype(jnp.int32), axis=1)
    folds = rank[:, None] == (ends - 1)[None, :]
    block_bias = jnp.log((BLOCK + 1 - sizes).astype(jnp.float32))
    packed_bias = jnp.sum(jnp.where(folds, block_bias[None, :], 0.0), axis=1).astype(jnp.bfloat16)
    owner = jnp.sum((block[:, None] >= request_ends[None, :]).astype(jnp.int32), axis=1)
    packed_request = jnp.where(rank < ends[-1], owner, -1)

    heads = geo.heads
    peak_score, softmax_total = part[..., HD], part[..., HD + LANES // 2]
    weighted = part[..., :HD]
    score_scale = 1.0 / jnp.sqrt(jnp.float32(HD))
    query_heads = queries.reshape(req_count, heads, HD)
    own_score = (
        jnp.einsum(
            "rhd,rhd->hr",
            query_heads,
            new_keys.reshape(req_count, heads, HD),
            preferred_element_type=jnp.float32,
        )
        * score_scale
    )
    final_peak = jnp.maximum(peak_score, own_score)
    rescale_old = jnp.exp(peak_score - final_peak)
    own_prob = jnp.exp(own_score - final_peak)
    new_value_heads = jnp.transpose(new_values.reshape(req_count, heads, HD), (1, 0, 2)).astype(
        jnp.float32
    )
    softmax_total = softmax_total * rescale_old + own_prob
    weighted = weighted * rescale_old[:, :, None] + own_prob[:, :, None] * new_value_heads
    attention_heads = weighted / softmax_total[:, :, None]
    attention = (
        jnp.transpose(attention_heads, (1, 0, 2))
        .reshape(req_count, heads * HD)
        .astype(jnp.bfloat16)
    )
    partial_output = jnp.dot(attention, out_weight, preferred_element_type=jnp.float32)
    layer_output = lax.psum_scatter(partial_output, "tp", scatter_dimension=0, tiled=True).astype(
        jnp.bfloat16
    )
    return (packed_keys, packed_values, packed_bias, packed_request, layer_output)


def solution(mesh):
    in_specs = (
        P("seq", "tp"),
        P("seq", "tp"),
        P("seq"),
        P("seq"),
        P(),
        P(None, "tp"),
        P(None, "tp"),
        P(None, "tp"),
        P("tp", "seq"),
    )
    out_specs = (P("seq", "tp"), P("seq", "tp"), P("seq"), P("seq"), P("tp", "seq"))
    return jax.shard_map(
        on_device, mesh=mesh, in_specs=in_specs, out_specs=out_specs, check_vma=False
    )
```

```python
import functools

import jax
import jax.numpy as jnp
from jax import lax
from jax.experimental import pallas as pl
from jax.experimental.pallas import tpu as pltpu
from jax.sharding import PartitionSpec as P

HD = 256
BLOCK = 128
LANES = 128
SUB = 16
LEAST_KEPT = BLOCK // 4
MOST_KEPT = BLOCK // 2
LOW = -1e30
VMEM_LIMIT = 56 * 1024 * 1024
VMEM_SMALL = 24 * 1024 * 1024


class Geometry:
    def __init__(self, peers, blocks, features):
        self.peers = peers
        self.blocks = blocks
        self.features = features
        self.heads = features // HD
        self.slots = blocks * (MOST_KEPT + 1)
        self.peer_rows = -(-self.slots // peers)
        self.groups = self.peer_rows // SUB
        self.main = self.groups * SUB
        self.chunks = 2 * features // LANES
        self.tail = -(-self.chunks // SUB) * SUB
        self.share = self.chunks // 2 * self.main
        self.group_rows = SUB * peers
        assert self.peer_rows == self.main + 1
        assert self.block_range(self.main * peers, self.slots - 1) == (blocks - 1, blocks)
        self.join = min(peers, max(1, 256 // self.main))
        self.joins = peers // self.join
        window = self.join * self.peer_rows + SUB - 1
        self.window = min(-(-window // SUB) * SUB, self.slots)
        assert self.slots % SUB == 0 and peers % self.join == 0

    def block_range(self, first, last):
        low = max(0, -(-(first - MOST_KEPT) // (MOST_KEPT + 1)))
        high = min(self.blocks - 1, last // (LEAST_KEPT + 1))
        return low, high + 1

    def ranges(self):
        rows = self.group_rows
        return [self.block_range(g * rows, (g + 1) * rows - 1) for g in range(self.groups)]

    def places(self):
        places = [0]
        for low, high in self.ranges():
            places.append(places[-1] + (high - low) * BLOCK)
        return places


def iota(shape, axis):
    return lax.broadcasted_iota(jnp.int32, shape, axis)


def dot(a, b, contract=((1,), (0,))):
    return lax.dot_general(a, b, (contract, ((), ())), preferred_element_type=jnp.float32)


def pack_kernel(geo, tails, keep_ref, weight_ref, cache_ref, *refs):
    step = pl.program_id(0)
    blocks, peers = geo.blocks, geo.peers
    if tails:
        end_refs, (main_ref, tail_ref, pick_ref, scale_ref) = refs[:2], refs[2:]
    else:
        main_ref, pick_ref, scale_ref = refs
    ranges = geo.ranges()
    places = geo.places()

    def flags():
        keep = keep_ref[...].reshape(blocks, BLOCK).astype(jnp.float32)
        weight = weight_ref[...].reshape(blocks, BLOCK).astype(jnp.float32)
        return keep, weight * (1.0 - keep)

    @pl.when(step == 0)
    def _():
        keep, dropped = flags()
        kept = jnp.sum(keep, axis=1, keepdims=True)
        inverse = 1.0 / jnp.sum(dropped, axis=1, keepdims=True)
        earlier = (iota((BLOCK, BLOCK), 0) < iota((BLOCK, BLOCK), 1)).astype(jnp.bfloat16)
        within = dot(keep.astype(jnp.bfloat16), earlier)
        before = (iota((blocks, blocks), 1) < iota((blocks, blocks), 0)).astype(jnp.bfloat16)
        sizes = jnp.broadcast_to(kept + 1.0, (blocks, BLOCK)).astype(jnp.bfloat16)
        base = dot(before, sizes)
        entry = jnp.where(keep > 0.0, base + within, -1.0).astype(jnp.int32)
        fold_entry = (base + kept).astype(jnp.int32)

        def select(index, low, high):
            scale = jnp.ones(index.shape, jnp.float32)
            picks = []
            for b in range(low, high):
                folds = index == fold_entry[b : b + 1, :]
                one = jnp.where(index == entry[b : b + 1, :], 1.0, 0.0)
                picked = jnp.where(folds, dropped[b : b + 1, :], one)
                picks.append(picked.astype(jnp.bfloat16))
                scale = jnp.where(folds, inverse[b : b + 1, :], scale)
            return picks, scale

        row = iota((geo.group_rows, BLOCK), 0)
        for g in range(geo.groups):
            index = (g * SUB + row % SUB) * peers + row // SUB
            picks, scale_ref[g, :, :] = select(index, *ranges[g])
            for i, picked in enumerate(picks):
                at = places[g] + i * BLOCK
                pick_ref[:, at : at + BLOCK] = picked
        if tails:
            index = geo.main * peers + iota((peers, BLOCK), 0)
            (picked,), scale = select(index, blocks - 1, blocks)
            left = []
            for end_ref in end_refs:
                rows = dot(picked, end_ref[...])
                for c in range(geo.chunks // 2):
                    left.append((rows[:, c * LANES : (c + 1) * LANES] * scale).astype(jnp.bfloat16))
            shape = (peers * geo.tail, geo.chunks * peers)
            row, col = iota(shape, 0), iota(shape, 1)
            wanted = row % geo.tail * peers + row // geo.tail
            turn = jnp.where(wanted == col, 1.0, 0.0).astype(jnp.bfloat16)
            rows = dot(turn, jnp.concatenate(left, axis=0)).astype(jnp.bfloat16)
            tail_ref[...] = rows.reshape(peers, geo.tail, LANES)

    for g in range(geo.groups):
        low, high = ranges[g]
        rows = dot(
            pick_ref[:, places[g] : places[g] + (high - low) * BLOCK],
            cache_ref[low * BLOCK : high * BLOCK, :],
        )
        for half in range(HD // LANES):
            chunk = rows[:, half * LANES : (half + 1) * LANES] * scale_ref[g]
            chunk = chunk.astype(jnp.bfloat16).reshape(peers, SUB, LANES)
            at = half * geo.main + g * SUB
            main_ref[:, at : at + SUB, :] = chunk


def attend_kernel(
    geo, keep_ref, weight_ref, first_ref, last_ref, query_ref, key_ref, value_ref,
    part_ref, fold_ref,
):
    step = pl.program_id(0)
    blocks = geo.blocks
    keep = keep_ref[...].reshape(blocks, BLOCK).astype(jnp.float32)
    weight = weight_ref[...].reshape(blocks, BLOCK).astype(jnp.float32)
    dropped = weight * (1.0 - keep)
    inverse = 1.0 / jnp.sum(dropped, axis=1, keepdims=True)

    @pl.when(step == 0)
    def _():
        for b in range(blocks):
            mine = iota((blocks, BLOCK), 0) == b
            fold_ref[:, b * BLOCK : (b + 1) * BLOCK] = jnp.where(
                mine, dropped[b : b + 1, :], 0.0
            ).astype(jnp.bfloat16)

    query = query_ref[...]
    first, last = first_ref[...], last_ref[...]
    requests = query.shape[0]
    score_scale = HD**-0.5
    folded_keys = (dot(fold_ref[...], key_ref[...]) * inverse).astype(jnp.bfloat16)
    folded_values = (dot(fold_ref[...], value_ref[...]) * inverse).astype(jnp.bfloat16)
    ones = jnp.ones((8, BLOCK), jnp.bfloat16)
    kept_lanes = dot(ones, keep.astype(jnp.bfloat16), ((1,), (1,)))[0:1, :]
    bias = jnp.log(BLOCK - kept_lanes).astype(jnp.bfloat16).astype(jnp.float32)
    fold_scores = dot(query, folded_keys, ((1,), (1,))) * score_scale + bias
    block = iota((requests, blocks), 1)
    fold_member = (block >= first) & (block < last)
    fold_scores = jnp.where(fold_member, fold_scores, LOW)
    scores = dot(query, key_ref[...], ((1,), (1,))) * score_scale
    lane_block = iota((requests, blocks * BLOCK), 1) // BLOCK
    kept_rows = jnp.concatenate(
        [jnp.broadcast_to(keep[b : b + 1, :], (requests, BLOCK)) for b in range(blocks)], axis=1
    )
    member = (lane_block >= first) & (lane_block < last) & (kept_rows > 0.0)
    scores = jnp.where(member, scores, LOW)
    peak = jnp.maximum(
        jnp.max(scores, axis=1, keepdims=True), jnp.max(fold_scores, axis=1, keepdims=True)
    )
    peak = peak.astype(jnp.bfloat16).astype(jnp.float32)
    probs = jnp.where(member, jnp.exp(scores - peak), 0.0)
    fold_probs = jnp.where(fold_member, jnp.exp(fold_scores - peak), 0.0)
    total = jnp.sum(probs, axis=1, keepdims=True) + jnp.sum(fold_probs, axis=1, keepdims=True)
    mixed = dot(probs.astype(jnp.bfloat16), value_ref[...]) + dot(
        fold_probs.astype(jnp.bfloat16), folded_values
    )
    part_ref[0, :, 0:HD] = mixed
    part_ref[0, :, HD:] = jnp.where(iota((requests, LANES), 1) < LANES // 2, peak, total)


def whole(*shape):
    return pl.BlockSpec(shape, lambda t: (0,) * len(shape))


def pack(geo, keep, weight, cache, ends=()):
    rows = cache.shape[0]
    width = geo.places()[-1]
    end_block = geo.blocks - 1
    out_specs = [pl.BlockSpec((geo.peers, 2 * geo.main, LANES), lambda t: (0, t, 0))]
    out_shape = [jax.ShapeDtypeStruct((geo.peers, geo.share, LANES), jnp.bfloat16)]
    if ends:
        out_specs.append(whole(geo.peers, geo.tail, LANES))
        out_shape.append(jax.ShapeDtypeStruct((geo.peers, geo.tail, LANES), jnp.bfloat16))
    return pl.pallas_call(
        functools.partial(pack_kernel, geo, bool(ends)),
        grid=(geo.heads,),
        in_specs=[whole(rows), whole(rows), pl.BlockSpec((rows, HD), lambda t: (0, t))]
        + [pl.BlockSpec((BLOCK, geo.features), lambda t: (end_block, 0))] * len(ends),
        out_specs=out_specs,
        out_shape=out_shape,
        scratch_shapes=[
            pltpu.VMEM((geo.group_rows, width), jnp.bfloat16),
            pltpu.VMEM((geo.groups, geo.group_rows, BLOCK), jnp.float32),
        ],
        compiler_params=pltpu.CompilerParams(vmem_limit_bytes=VMEM_LIMIT),
        cost_estimate=pl.CostEstimate(
            flops=2 * geo.group_rows * width * geo.features,
            bytes_accessed=3 * rows * geo.features,
            transcendentals=0,
        ),
    )(keep, weight, cache, *ends)


def attend(geo, keep, weight, first, last, queries, cache_keys, cache_values):
    rows = cache_keys.shape[0]
    requests = queries.shape[0]
    return pl.pallas_call(
        functools.partial(attend_kernel, geo),
        grid=(geo.heads,),
        in_specs=[
            whole(rows),
            whole(rows),
            whole(requests, 1),
            whole(requests, 1),
            pl.BlockSpec((requests, HD), lambda t: (0, t)),
            pl.BlockSpec((rows, HD), lambda t: (0, t)),
            pl.BlockSpec((rows, HD), lambda t: (0, t)),
        ],
        out_specs=pl.BlockSpec((1, requests, HD + LANES), lambda t: (t, 0, 0)),
        out_shape=jax.ShapeDtypeStruct((geo.heads, requests, HD + LANES), jnp.float32),
        scratch_shapes=[pltpu.VMEM((geo.blocks, rows), jnp.bfloat16)],
        compiler_params=pltpu.CompilerParams(vmem_limit_bytes=VMEM_LIMIT),
        cost_estimate=pl.CostEstimate(
            flops=8 * rows * requests * geo.features,
            bytes_accessed=2 * rows * geo.features * 2,
            transcendentals=rows * requests * geo.heads,
        ),
    )(keep, weight, first, last, queries, cache_keys, cache_values)


def my_start(kept, me):
    return jnp.sum(jnp.where(iota(kept.shape, 0) < me, kept + 1, 0))


def turn_kernel(geo, kept_ref, *refs):
    main_ref, tail_refs = refs[0], refs[1:-6]
    sent_ref, counts_ref, held_ref, counts_sem, in_sems, out_sems = refs[-6:]
    counts = pltpu.make_async_copy(kept_ref, counts_ref, counts_sem)
    counts.start()
    me = lax.axis_index("seq")
    peers, share = geo.peers, geo.share
    arrivals = []
    for p in range(peers):
        held = held_ref.at[p]
        copies = [pltpu.make_async_copy(main_ref.at[p], held.at[0:share], in_sems.at[0, p])]
        for tail_ref in tail_refs:
            tail = held.at[share : share + geo.tail]
            copies.append(pltpu.make_async_copy(tail_ref.at[p], tail, in_sems.at[1, p]))
        for copy in copies:
            copy.start()
        arrivals.append(copies)
    counts.wait()
    start = my_start(counts_ref[...], me)
    departures = []
    for p in range(peers):
        device = lax.rem(start + p, peers)
        for copy in arrivals[p]:
            copy.wait()
        departures.append(
            pltpu.make_async_copy(held_ref.at[p], sent_ref.at[device], out_sems.at[p])
        )
        departures[p].start()
    for copy in departures:
        copy.wait()


def turn(geo, kept, main, tail=None):
    tails = [] if tail is None else [tail]
    shape = (geo.peers, geo.share + len(tails) * geo.tail, LANES)
    size = geo.peers * geo.share * LANES
    return pl.pallas_call(
        functools.partial(turn_kernel, geo),
        in_specs=[pl.BlockSpec(memory_space=pl.ANY)] * (2 + len(tails)),
        out_specs=pl.BlockSpec(memory_space=pl.ANY),
        out_shape=jax.ShapeDtypeStruct(shape, jnp.bfloat16),
        scratch_shapes=[
            pltpu.VMEM(kept.shape, jnp.int32),
            pltpu.VMEM(shape, jnp.bfloat16),
            pltpu.SemaphoreType.DMA,
            pltpu.SemaphoreType.DMA((2, geo.peers)),
            pltpu.SemaphoreType.DMA((geo.peers,)),
        ],
        compiler_params=pltpu.CompilerParams(vmem_limit_bytes=VMEM_LIMIT),
        cost_estimate=pl.CostEstimate(flops=0, bytes_accessed=4 * size, transcendentals=0),
    )(kept, main, *tails)


def low_slots(geo, slot_ref):
    lows = []
    for q in range(geo.joins):
        low = jnp.minimum(slot_ref[q * geo.join] // SUB * SUB, geo.slots - geo.window)
        lows.append(pl.multiple_of(low, SUB))
    return lows


def plan_kernel(geo, slot_ref, tail_ref, pick_ref, last_ref, keys_ref, values_ref):
    peers, main = geo.peers, geo.main
    width = geo.join * main
    lows = low_slots(geo, slot_ref)
    for q in range(geo.joins):
        lane = iota((1, width), 1)
        target = lane % main
        last = jnp.full((1, peers), -1, jnp.int32)
        for j in range(geo.join):
            at = slot_ref[q * geo.join + j] - lows[q]
            target = target + jnp.where(lane // main == j, at, 0)
            last = jnp.where(iota((1, peers), 1) == q * geo.join + j, at + main, last)
        picked = jnp.where(iota((geo.window, width), 0) == target, 1.0, 0.0)
        pick_ref[q, :, :] = picked.astype(jnp.bfloat16)
        picked = jnp.where(iota((geo.window, peers), 0) == last, 1.0, 0.0)
        last_ref[q, :, :] = picked.astype(jnp.bfloat16)
    tails = tail_ref[...].reshape(peers * geo.tail, LANES)
    share = geo.chunks // 2
    for part, out_ref in enumerate((keys_ref, values_ref)):
        shape = (share * peers, peers * geo.tail)
        row, col = iota(shape, 0), iota(shape, 1)
        wanted = row % peers * geo.tail + row // peers + part * share
        back = jnp.where(wanted == col, 1.0, 0.0).astype(jnp.bfloat16)
        rows = dot(back, tails).astype(jnp.bfloat16)
        for c in range(share):
            at = c * LANES
            out_ref[:, at : at + LANES] = rows[c * peers : (c + 1) * peers, :]


def plan(geo, slot, slabs):
    tail_block = geo.share // geo.tail
    picks = [(geo.joins, geo.window, n) for n in (geo.join * geo.main, geo.peers)]
    shapes = picks + [(geo.peers, geo.features)] * 2
    return pl.pallas_call(
        functools.partial(plan_kernel, geo),
        grid=(1,),
        in_specs=[
            pl.BlockSpec(memory_space=pltpu.SMEM),
            pl.BlockSpec((geo.peers, geo.tail, LANES), lambda t: (0, tail_block, 0)),
        ],
        out_specs=[whole(*shape) for shape in shapes],
        out_shape=[jax.ShapeDtypeStruct(shape, jnp.bfloat16) for shape in shapes],
        compiler_params=pltpu.CompilerParams(vmem_limit_bytes=VMEM_SMALL),
    )(slot, slabs)


def unpack_kernel(geo, slot_ref, slab_ref, pick_ref, last_ref, tail_ref, out_ref):
    main = geo.main
    width = geo.join * main
    lows = low_slots(geo, slot_ref)
    out_ref[...] = jnp.zeros_like(out_ref)
    for q in range(geo.joins):
        sources = slice(q * geo.join, (q + 1) * geo.join)
        rows = [
            slab_ref[sources, c * main : (c + 1) * main, :].reshape(width, LANES)
            for c in range(out_ref.shape[1] // LANES)
        ]
        placed = dot(pick_ref[q], jnp.concatenate(rows, axis=1))
        placed = placed + dot(last_ref[q], tail_ref[...])
        out_ref[pl.ds(lows[q], geo.window), :] += placed.astype(jnp.bfloat16)


def unpack(geo, slot, slabs, pick, last, tail):
    tile = HD * (2 if geo.heads % 2 == 0 else 1)
    tile_rows = tile // LANES * geo.main
    return pl.pallas_call(
        functools.partial(unpack_kernel, geo),
        grid=(geo.features // tile,),
        in_specs=[
            pl.BlockSpec(memory_space=pltpu.SMEM),
            pl.BlockSpec((geo.peers, tile_rows, LANES), lambda t: (0, t, 0)),
            whole(*pick.shape),
            whole(*last.shape),
            pl.BlockSpec((geo.peers, tile), lambda t: (0, t)),
        ],
        out_specs=pl.BlockSpec((geo.slots, tile), lambda t: (0, t)),
        out_shape=jax.ShapeDtypeStruct((geo.slots, geo.features), jnp.bfloat16),
        compiler_params=pltpu.CompilerParams(vmem_limit_bytes=VMEM_SMALL),
        cost_estimate=pl.CostEstimate(
            flops=2 * geo.joins * geo.window * 256 * geo.features,
            bytes_accessed=4 * geo.peers * geo.share * LANES,
            transcendentals=0,
        ),
    )(slot, slabs, pick, last, tail)


def merge(one, two):
    half = HD + LANES // 2
    peak_one, peak_two = one[..., HD : HD + 1], two[..., HD : HD + 1]
    peak = jnp.maximum(peak_one, peak_two)
    rescale_one, rescale_two = jnp.exp(peak_one - peak), jnp.exp(peak_two - peak)
    mixed = one * rescale_one + two * rescale_two
    lane = lax.broadcasted_iota(jnp.int32, one.shape, len(one.shape) - 1)
    return jnp.where((lane >= HD) & (lane < half), peak, mixed)


def narrow(part):
    lane = lax.broadcasted_iota(jnp.int32, part.shape, len(part.shape) - 1)
    high = part.astype(jnp.bfloat16)
    low = (part - high.astype(jnp.float32)).astype(jnp.bfloat16)
    return jnp.where(lane < HD + LANES * 3 // 4, high, low)


def widen(part):
    total = HD + LANES // 2
    part = part.astype(jnp.float32)
    lane = lax.broadcasted_iota(jnp.int32, part.shape, len(part.shape) - 1)
    both = part[..., total : total + 1] + part[..., -1:]
    return jnp.where(lane >= total, both, part)


def on_device(
    cache_keys, cache_values, keep_flags, drop_weight, req_blocks, queries, new_keys, new_values,
    out_weight,
):
    peers = lax.axis_size("seq")
    me = lax.axis_index("seq")
    row_count, features = cache_keys.shape
    block_count = row_count // BLOCK
    geo = Geometry(peers, block_count, features)
    req_count = queries.shape[0]
    kept_count = jnp.sum(keep_flags.reshape(block_count, BLOCK), axis=1)
    kept_all = lax.all_to_all(
        jnp.broadcast_to(kept_count[None, :], (peers, block_count)),
        "seq", split_axis=0, concat_axis=0, tiled=True,
    )

    main, tail = pack(geo, keep_flags, drop_weight, cache_keys, (cache_keys, cache_values))
    sent = turn(geo, kept_all, main, tail)
    tied = (sent, keep_flags, drop_weight, kept_all, req_blocks)
    sent, keep_flags, drop_weight, kept_all, req_blocks = lax.optimization_barrier(tied)
    keys = lax.all_to_all(sent, "seq", split_axis=0, concat_axis=0, tiled=True)

    request_ends = jnp.cumsum(req_blocks)
    first = (request_ends - req_blocks - me * block_count)[:, None]
    last = (request_ends - me * block_count)[:, None]
    part = attend(geo, keep_flags, drop_weight, first, last, queries, cache_keys, cache_values)
    (main,) = pack(geo, keep_flags, drop_weight, cache_values)
    sent = turn(geo, kept_all, main)
    distance = 1
    while distance < peers:
        if distance == peers // 2:
            part, sent = lax.optimization_barrier((part, sent))
        pairs = [(i, i ^ distance) for i in range(peers)]
        if distance == peers // 2:
            part = merge(part, widen(lax.ppermute(narrow(part), "seq", pairs)))
        else:
            part = merge(part, lax.ppermute(part, "seq", pairs))
        distance *= 2
    part, sent = lax.optimization_barrier((part, sent))
    values = lax.all_to_all(sent, "seq", split_axis=0, concat_axis=0, tiled=True)

    counts = jnp.sum(kept_all, axis=1) + block_count
    starts = jnp.cumsum(counts) - counts
    slot = (starts + (me - starts) % peers) // peers
    pick, last, key_tails, value_tails = plan(geo, slot, keys)
    packed_keys = unpack(geo, slot, keys, pick, last, key_tails)
    packed_values = unpack(geo, slot, values, pick, last, value_tails)

    sizes = kept_all.reshape(-1) + 1
    ends = jnp.cumsum(sizes)
    rank = jnp.arange(geo.slots, dtype=jnp.int32) * peers + me
    block = jnp.sum((rank[:, None] >= ends[None, :]).astype(jnp.int32), axis=1)
    folds = rank[:, None] == (ends - 1)[None, :]
    block_bias = jnp.log((BLOCK + 1 - sizes).astype(jnp.float32))
    packed_bias = jnp.sum(jnp.where(folds, block_bias[None, :], 0.0), axis=1).astype(jnp.bfloat16)
    owner = jnp.sum((block[:, None] >= request_ends[None, :]).astype(jnp.int32), axis=1)
    packed_request = jnp.where(rank < ends[-1], owner, -1)

    heads = geo.heads
    peak_score, softmax_total = part[..., HD], part[..., HD + LANES // 2]
    weighted = part[..., :HD]
    score_scale = 1.0 / jnp.sqrt(jnp.float32(HD))
    query_heads = queries.reshape(req_count, heads, HD)
    own_score = (
        jnp.einsum(
            "rhd,rhd->hr",
            query_heads,
            new_keys.reshape(req_count, heads, HD),
            preferred_element_type=jnp.float32,
        )
        * score_scale
    )
    final_peak = jnp.maximum(peak_score, own_score)
    rescale_old = jnp.exp(peak_score - final_peak)
    own_prob = jnp.exp(own_score - final_peak)
    new_value_heads = jnp.transpose(new_values.reshape(req_count, heads, HD), (1, 0, 2)).astype(
        jnp.float32
    )
    softmax_total = softmax_total * rescale_old + own_prob
    weighted = weighted * rescale_old[:, :, None] + own_prob[:, :, None] * new_value_heads
    attention_heads = weighted / softmax_total[:, :, None]
    attention = (
        jnp.transpose(attention_heads, (1, 0, 2))
        .reshape(req_count, heads * HD)
        .astype(jnp.bfloat16)
    )
    partial_output = jnp.dot(attention, out_weight, preferred_element_type=jnp.float32)
    layer_output = lax.psum_scatter(partial_output, "tp", scatter_dimension=0, tiled=True).astype(
        jnp.bfloat16
    )
    return (packed_keys, packed_values, packed_bias, packed_request, layer_output)


def solution(mesh):
    in_specs = (
        P("seq", "tp"),
        P("seq", "tp"),
        P("seq"),
        P("seq"),
        P(),
        P(None, "tp"),
        P(None, "tp"),
        P(None, "tp"),
        P("tp", "seq"),
    )
    out_specs = (P("seq", "tp"), P("seq", "tp"), P("seq"), P("seq"), P("tp", "seq"))
    return jax.shard_map(
        on_device, mesh=mesh, in_specs=in_specs, out_specs=out_specs, check_vma=False
    )
```

```python
import functools

import jax
import jax.numpy as jnp
from jax import lax
from jax.experimental import pallas as pl
from jax.experimental.pallas import tpu as pltpu
from jax.sharding import PartitionSpec as P

HD = 256
BLOCK = 128
LANES = 128
SUB = 16
LEAST_KEPT = BLOCK // 4
MOST_KEPT = BLOCK // 2
LOW = -1e30
VMEM_LIMIT = 56 * 1024 * 1024
TURNS = 4
VMEM_SMALL = 24 * 1024 * 1024


class Geometry:
    def __init__(self, peers, blocks, features):
        self.peers = peers
        self.blocks = blocks
        self.features = features
        self.heads = features // HD
        self.slots = blocks * (MOST_KEPT + 1)
        self.peer_rows = -(-self.slots // peers)
        self.groups = self.peer_rows // SUB
        self.main = self.groups * SUB
        self.chunks = 2 * features // LANES
        self.tail = -(-self.chunks // SUB) * SUB
        self.share = self.chunks // 2 * self.main
        self.group_rows = SUB * peers
        assert self.peer_rows == self.main + 1
        assert self.block_range(self.main * peers, self.slots - 1) == (blocks - 1, blocks)
        self.join = min(peers, max(1, 256 // self.main))
        self.joins = peers // self.join
        window = self.join * self.peer_rows + SUB - 1
        self.window = min(-(-window // SUB) * SUB, self.slots)
        assert self.slots % SUB == 0 and peers % self.join == 0

    def block_range(self, first, last):
        low = max(0, -(-(first - MOST_KEPT) // (MOST_KEPT + 1)))
        high = min(self.blocks - 1, last // (LEAST_KEPT + 1))
        return low, high + 1

    def ranges(self):
        rows = self.group_rows
        return [self.block_range(g * rows, (g + 1) * rows - 1) for g in range(self.groups)]

    def places(self):
        places = [0]
        for low, high in self.ranges():
            places.append(places[-1] + (high - low) * BLOCK)
        return places


def iota(shape, axis):
    return lax.broadcasted_iota(jnp.int32, shape, axis)


def dot(a, b, contract=((1,), (0,))):
    return lax.dot_general(a, b, (contract, ((), ())), preferred_element_type=jnp.float32)


def pack_kernel(geo, tails, keep_ref, weight_ref, cache_ref, *refs):
    step = pl.program_id(0)
    blocks, peers = geo.blocks, geo.peers
    if tails:
        end_refs, (main_ref, tail_ref, pick_ref, scale_ref) = refs[:2], refs[2:]
    else:
        main_ref, pick_ref, scale_ref = refs
    ranges = geo.ranges()
    places = geo.places()

    def flags():
        keep = keep_ref[...].reshape(blocks, BLOCK).astype(jnp.float32)
        weight = weight_ref[...].reshape(blocks, BLOCK).astype(jnp.float32)
        return keep, weight * (1.0 - keep)

    @pl.when(step == 0)
    def _():
        keep, dropped = flags()
        kept = jnp.sum(keep, axis=1, keepdims=True)
        inverse = 1.0 / jnp.sum(dropped, axis=1, keepdims=True)
        earlier = (iota((BLOCK, BLOCK), 0) < iota((BLOCK, BLOCK), 1)).astype(jnp.bfloat16)
        within = dot(keep.astype(jnp.bfloat16), earlier)
        before = (iota((blocks, blocks), 1) < iota((blocks, blocks), 0)).astype(jnp.bfloat16)
        sizes = jnp.broadcast_to(kept + 1.0, (blocks, BLOCK)).astype(jnp.bfloat16)
        base = dot(before, sizes)
        entry = jnp.where(keep > 0.0, base + within, -1.0).astype(jnp.int32)
        fold_entry = (base + kept).astype(jnp.int32)

        def select(index, low, high):
            scale = jnp.ones(index.shape, jnp.float32)
            picks = []
            for b in range(low, high):
                folds = index == fold_entry[b : b + 1, :]
                one = jnp.where(index == entry[b : b + 1, :], 1.0, 0.0)
                picked = jnp.where(folds, dropped[b : b + 1, :], one)
                picks.append(picked.astype(jnp.bfloat16))
                scale = jnp.where(folds, inverse[b : b + 1, :], scale)
            return picks, scale

        row = iota((geo.group_rows, BLOCK), 0)
        for g in range(geo.groups):
            index = (g * SUB + row % SUB) * peers + row // SUB
            picks, scale_ref[g, :, :] = select(index, *ranges[g])
            for i, picked in enumerate(picks):
                at = places[g] + i * BLOCK
                pick_ref[:, at : at + BLOCK] = picked
        if tails:
            index = geo.main * peers + iota((peers, BLOCK), 0)
            (picked,), scale = select(index, blocks - 1, blocks)
            left = []
            for end_ref in end_refs:
                rows = dot(picked, end_ref[...])
                for c in range(geo.chunks // 2):
                    left.append((rows[:, c * LANES : (c + 1) * LANES] * scale).astype(jnp.bfloat16))
            shape = (peers * geo.tail, geo.chunks * peers)
            row, col = iota(shape, 0), iota(shape, 1)
            wanted = row % geo.tail * peers + row // geo.tail
            turn = jnp.where(wanted == col, 1.0, 0.0).astype(jnp.bfloat16)
            rows = dot(turn, jnp.concatenate(left, axis=0)).astype(jnp.bfloat16)
            tail_ref[...] = rows.reshape(peers, geo.tail, LANES)

    for g in range(geo.groups):
        low, high = ranges[g]
        rows = dot(
            pick_ref[:, places[g] : places[g] + (high - low) * BLOCK],
            cache_ref[low * BLOCK : high * BLOCK, :],
        )
        for half in range(HD // LANES):
            chunk = rows[:, half * LANES : (half + 1) * LANES] * scale_ref[g]
            chunk = chunk.astype(jnp.bfloat16).reshape(peers, SUB, LANES)
            at = half * geo.main + g * SUB
            main_ref[:, at : at + SUB, :] = chunk


def attend_kernel(
    geo, keep_ref, weight_ref, first_ref, last_ref, query_ref, key_ref, value_ref,
    part_ref, fold_ref,
):
    step = pl.program_id(0)
    blocks = geo.blocks
    keep = keep_ref[...].reshape(blocks, BLOCK).astype(jnp.float32)
    weight = weight_ref[...].reshape(blocks, BLOCK).astype(jnp.float32)
    dropped = weight * (1.0 - keep)
    inverse = 1.0 / jnp.sum(dropped, axis=1, keepdims=True)

    @pl.when(step == 0)
    def _():
        for b in range(blocks):
            mine = iota((blocks, BLOCK), 0) == b
            fold_ref[:, b * BLOCK : (b + 1) * BLOCK] = jnp.where(
                mine, dropped[b : b + 1, :], 0.0
            ).astype(jnp.bfloat16)

    query = query_ref[...]
    first, last = first_ref[...], last_ref[...]
    requests = query.shape[0]
    score_scale = HD**-0.5
    folded_keys = (dot(fold_ref[...], key_ref[...]) * inverse).astype(jnp.bfloat16)
    folded_values = (dot(fold_ref[...], value_ref[...]) * inverse).astype(jnp.bfloat16)
    ones = jnp.ones((8, BLOCK), jnp.bfloat16)
    kept_lanes = dot(ones, keep.astype(jnp.bfloat16), ((1,), (1,)))[0:1, :]
    bias = jnp.log(BLOCK - kept_lanes).astype(jnp.bfloat16).astype(jnp.float32)
    fold_scores = dot(query, folded_keys, ((1,), (1,))) * score_scale + bias
    block = iota((requests, blocks), 1)
    fold_member = (block >= first) & (block < last)
    fold_scores = jnp.where(fold_member, fold_scores, LOW)
    scores = dot(query, key_ref[...], ((1,), (1,))) * score_scale
    lane_block = iota((requests, blocks * BLOCK), 1) // BLOCK
    kept_rows = jnp.concatenate(
        [jnp.broadcast_to(keep[b : b + 1, :], (requests, BLOCK)) for b in range(blocks)], axis=1
    )
    member = (lane_block >= first) & (lane_block < last) & (kept_rows > 0.0)
    scores = jnp.where(member, scores, LOW)
    peak = jnp.maximum(
        jnp.max(scores, axis=1, keepdims=True), jnp.max(fold_scores, axis=1, keepdims=True)
    )
    probs = jnp.where(member, jnp.exp(scores - peak), 0.0)
    fold_probs = jnp.where(fold_member, jnp.exp(fold_scores - peak), 0.0)
    total = jnp.sum(probs, axis=1, keepdims=True) + jnp.sum(fold_probs, axis=1, keepdims=True)
    mixed = dot(probs.astype(jnp.bfloat16), value_ref[...]) + dot(
        fold_probs.astype(jnp.bfloat16), folded_values
    )
    part_ref[0, :, 0:HD] = mixed
    part_ref[0, :, HD:] = jnp.where(iota((requests, LANES), 1) < LANES // 2, peak, total)


def whole(*shape):
    return pl.BlockSpec(shape, lambda t: (0,) * len(shape))


def pack(geo, keep, weight, cache, ends=()):
    rows = cache.shape[0]
    width = geo.places()[-1]
    end_block = geo.blocks - 1
    out_specs = [pl.BlockSpec((geo.peers, 2 * geo.main, LANES), lambda t: (0, t, 0))]
    out_shape = [jax.ShapeDtypeStruct((geo.peers, geo.share, LANES), jnp.bfloat16)]
    if ends:
        out_specs.append(whole(geo.peers, geo.tail, LANES))
        out_shape.append(jax.ShapeDtypeStruct((geo.peers, geo.tail, LANES), jnp.bfloat16))
    return pl.pallas_call(
        functools.partial(pack_kernel, geo, bool(ends)),
        grid=(geo.heads,),
        in_specs=[whole(rows), whole(rows), pl.BlockSpec((rows, HD), lambda t: (0, t))]
        + [pl.BlockSpec((BLOCK, geo.features), lambda t: (end_block, 0))] * len(ends),
        out_specs=out_specs,
        out_shape=out_shape,
        scratch_shapes=[
            pltpu.VMEM((geo.group_rows, width), jnp.bfloat16),
            pltpu.VMEM((geo.groups, geo.group_rows, BLOCK), jnp.float32),
        ],
        compiler_params=pltpu.CompilerParams(vmem_limit_bytes=VMEM_LIMIT),
        cost_estimate=pl.CostEstimate(
            flops=2 * geo.group_rows * width * geo.features,
            bytes_accessed=3 * rows * geo.features,
            transcendentals=0,
        ),
    )(keep, weight, cache, *ends)


def attend(geo, keep, weight, first, last, queries, cache_keys, cache_values):
    rows = cache_keys.shape[0]
    requests = queries.shape[0]
    return pl.pallas_call(
        functools.partial(attend_kernel, geo),
        grid=(geo.heads,),
        in_specs=[
            whole(rows),
            whole(rows),
            whole(requests, 1),
            whole(requests, 1),
            pl.BlockSpec((requests, HD), lambda t: (0, t)),
            pl.BlockSpec((rows, HD), lambda t: (0, t)),
            pl.BlockSpec((rows, HD), lambda t: (0, t)),
        ],
        out_specs=pl.BlockSpec((1, requests, HD + LANES), lambda t: (t, 0, 0)),
        out_shape=jax.ShapeDtypeStruct((geo.heads, requests, HD + LANES), jnp.float32),
        scratch_shapes=[pltpu.VMEM((geo.blocks, rows), jnp.bfloat16)],
        compiler_params=pltpu.CompilerParams(vmem_limit_bytes=VMEM_LIMIT),
        cost_estimate=pl.CostEstimate(
            flops=8 * rows * requests * geo.features,
            bytes_accessed=2 * rows * geo.features * 2,
            transcendentals=rows * requests * geo.heads,
        ),
    )(keep, weight, first, last, queries, cache_keys, cache_values)


def my_start(kept, me):
    return jnp.sum(jnp.where(iota(kept.shape, 0) < me, kept + 1, 0))


def turn_kernel(geo, kept_ref, *refs):
    main_ref, tail_refs = refs[0], refs[1:-7]
    sent_ref, counts_ref, held_ref, counts_sem, main_sems, tail_sem, out_sems = refs[-7:]
    me = lax.axis_index("seq")
    peers, share = geo.peers, geo.share
    counts = pltpu.make_async_copy(kept_ref, counts_ref, counts_sem)
    counts.start()
    tails = [
        pltpu.make_async_copy(ref, held_ref.at[:, share : share + geo.tail], tail_sem)
        for ref in tail_refs
    ]
    for copy in tails:
        copy.start()
    size = peers // TURNS
    mains = []
    for i in range(TURNS):
        some = slice(i * size, (i + 1) * size)
        mains.append(
            pltpu.make_async_copy(main_ref.at[some], held_ref.at[some, 0:share], main_sems.at[i])
        )
        mains[i].start()
    counts.wait()
    start = my_start(counts_ref[...], me)
    for copy in tails:
        copy.wait()
    departures = []
    for p in range(peers):
        if p % size == 0:
            mains[p // size].wait()
        device = lax.rem(start + p, peers)
        departures.append(
            pltpu.make_async_copy(held_ref.at[p], sent_ref.at[device], out_sems.at[p])
        )
        departures[p].start()
    for copy in departures:
        copy.wait()


def turn(geo, kept, main, tail=None):
    tails = [] if tail is None else [tail]
    shape = (geo.peers, geo.share + len(tails) * geo.tail, LANES)
    size = geo.peers * geo.share * LANES
    return pl.pallas_call(
        functools.partial(turn_kernel, geo),
        in_specs=[pl.BlockSpec(memory_space=pl.ANY)] * (2 + len(tails)),
        out_specs=pl.BlockSpec(memory_space=pl.ANY),
        out_shape=jax.ShapeDtypeStruct(shape, jnp.bfloat16),
        scratch_shapes=[
            pltpu.VMEM(kept.shape, jnp.int32),
            pltpu.VMEM(shape, jnp.bfloat16),
            pltpu.SemaphoreType.DMA,
            pltpu.SemaphoreType.DMA((TURNS,)),
            pltpu.SemaphoreType.DMA,
            pltpu.SemaphoreType.DMA((geo.peers,)),
        ],
        compiler_params=pltpu.CompilerParams(vmem_limit_bytes=VMEM_LIMIT),
        cost_estimate=pl.CostEstimate(flops=0, bytes_accessed=4 * size, transcendentals=0),
    )(kept, main, *tails)


def low_slots(geo, slot_ref):
    lows = []
    for q in range(geo.joins):
        low = jnp.minimum(slot_ref[q * geo.join] // SUB * SUB, geo.slots - geo.window)
        lows.append(pl.multiple_of(low, SUB))
    return lows


def plan_kernel(geo, slot_ref, tail_ref, pick_ref, last_ref, keys_ref, values_ref):
    peers, main = geo.peers, geo.main
    width = geo.join * main
    lows = low_slots(geo, slot_ref)
    for q in range(geo.joins):
        lane = iota((1, width), 1)
        target = lane % main
        last = jnp.full((1, peers), -1, jnp.int32)
        for j in range(geo.join):
            at = slot_ref[q * geo.join + j] - lows[q]
            target = target + jnp.where(lane // main == j, at, 0)
            last = jnp.where(iota((1, peers), 1) == q * geo.join + j, at + main, last)
        picked = jnp.where(iota((geo.window, width), 0) == target, 1.0, 0.0)
        pick_ref[q, :, :] = picked.astype(jnp.bfloat16)
        picked = jnp.where(iota((geo.window, peers), 0) == last, 1.0, 0.0)
        last_ref[q, :, :] = picked.astype(jnp.bfloat16)
    tails = tail_ref[...].reshape(peers * geo.tail, LANES)
    share = geo.chunks // 2
    for part, out_ref in enumerate((keys_ref, values_ref)):
        shape = (share * peers, peers * geo.tail)
        row, col = iota(shape, 0), iota(shape, 1)
        wanted = row % peers * geo.tail + row // peers + part * share
        back = jnp.where(wanted == col, 1.0, 0.0).astype(jnp.bfloat16)
        rows = dot(back, tails).astype(jnp.bfloat16)
        for c in range(share):
            at = c * LANES
            out_ref[:, at : at + LANES] = rows[c * peers : (c + 1) * peers, :]


def plan(geo, slot, slabs):
    tail_block = geo.share // geo.tail
    picks = [(geo.joins, geo.window, n) for n in (geo.join * geo.main, geo.peers)]
    shapes = picks + [(geo.peers, geo.features)] * 2
    return pl.pallas_call(
        functools.partial(plan_kernel, geo),
        grid=(1,),
        in_specs=[
            pl.BlockSpec(memory_space=pltpu.SMEM),
            pl.BlockSpec((geo.peers, geo.tail, LANES), lambda t: (0, tail_block, 0)),
        ],
        out_specs=[whole(*shape) for shape in shapes],
        out_shape=[jax.ShapeDtypeStruct(shape, jnp.bfloat16) for shape in shapes],
        compiler_params=pltpu.CompilerParams(vmem_limit_bytes=VMEM_SMALL),
    )(slot, slabs)


def unpack_kernel(geo, slot_ref, slab_ref, pick_ref, last_ref, tail_ref, out_ref):
    main = geo.main
    width = geo.join * main
    lows = low_slots(geo, slot_ref)
    out_ref[...] = jnp.zeros_like(out_ref)
    for q in range(geo.joins):
        sources = slice(q * geo.join, (q + 1) * geo.join)
        rows = [
            slab_ref[sources, c * main : (c + 1) * main, :].reshape(width, LANES)
            for c in range(out_ref.shape[1] // LANES)
        ]
        placed = dot(pick_ref[q], jnp.concatenate(rows, axis=1))
        placed = placed + dot(last_ref[q], tail_ref[...])
        out_ref[pl.ds(lows[q], geo.window), :] += placed.astype(jnp.bfloat16)


def unpack(geo, slot, slabs, pick, last, tail):
    tile = HD * (2 if geo.heads % 2 == 0 else 1)
    tile_rows = tile // LANES * geo.main
    return pl.pallas_call(
        functools.partial(unpack_kernel, geo),
        grid=(geo.features // tile,),
        in_specs=[
            pl.BlockSpec(memory_space=pltpu.SMEM),
            pl.BlockSpec((geo.peers, tile_rows, LANES), lambda t: (0, t, 0)),
            whole(*pick.shape),
            whole(*last.shape),
            pl.BlockSpec((geo.peers, tile), lambda t: (0, t)),
        ],
        out_specs=pl.BlockSpec((geo.slots, tile), lambda t: (0, t)),
        out_shape=jax.ShapeDtypeStruct((geo.slots, geo.features), jnp.bfloat16),
        compiler_params=pltpu.CompilerParams(vmem_limit_bytes=VMEM_SMALL),
        cost_estimate=pl.CostEstimate(
            flops=2 * geo.joins * geo.window * 256 * geo.features,
            bytes_accessed=4 * geo.peers * geo.share * LANES,
            transcendentals=0,
        ),
    )(slot, slabs, pick, last, tail)


def merge(one, two):
    half = HD + LANES // 2
    peak_one, peak_two = one[..., HD : HD + 1], two[..., HD : HD + 1]
    peak = jnp.maximum(peak_one, peak_two)
    rescale_one, rescale_two = jnp.exp(peak_one - peak), jnp.exp(peak_two - peak)
    mixed = one * rescale_one + two * rescale_two
    lane = lax.broadcasted_iota(jnp.int32, one.shape, len(one.shape) - 1)
    return jnp.where((lane >= HD) & (lane < half), peak, mixed)


def narrow(part):
    peak, total = HD, HD + LANES // 2
    lane = lax.broadcasted_iota(jnp.int32, part.shape, len(part.shape) - 1)
    high = lax.reduce_precision(part, 8, 7)
    rest = part - high
    middle = lax.reduce_precision(rest, 8, 7)
    low = lax.reduce_precision(rest - middle, 8, 7)
    second = ((lane >= peak + 16) & (lane < peak + 32)) | (lane >= total + 16)
    third = (lane >= peak + 32) & (lane < total)
    return jnp.where(second, middle, jnp.where(third, low, high)).astype(jnp.bfloat16)


def widen(part):
    peak, total = HD, HD + LANES // 2
    part = part.astype(jnp.float32)
    lane = lax.broadcasted_iota(jnp.int32, part.shape, len(part.shape) - 1)
    peaks = part[..., peak : peak + 1] + part[..., peak + 16 : peak + 17]
    peaks = peaks + part[..., peak + 32 : peak + 33]
    totals = part[..., total : total + 1] + part[..., total + 16 : total + 17]
    return jnp.where(lane >= total, totals, jnp.where(lane >= peak, peaks, part))


def on_device(
    cache_keys, cache_values, keep_flags, drop_weight, req_blocks, queries, new_keys, new_values,
    out_weight,
):
    peers = lax.axis_size("seq")
    me = lax.axis_index("seq")
    row_count, features = cache_keys.shape
    block_count = row_count // BLOCK
    geo = Geometry(peers, block_count, features)
    req_count = queries.shape[0]
    kept_count = jnp.sum(keep_flags.reshape(block_count, BLOCK), axis=1)
    kept_all = lax.all_to_all(
        jnp.broadcast_to(kept_count[None, :], (peers, block_count)),
        "seq", split_axis=0, concat_axis=0, tiled=True,
    )

    main, tail = pack(geo, keep_flags, drop_weight, cache_keys, (cache_keys, cache_values))
    sent = turn(geo, kept_all, main, tail)
    tied = (sent, keep_flags, drop_weight, kept_all, req_blocks)
    sent, keep_flags, drop_weight, kept_all, req_blocks = lax.optimization_barrier(tied)
    keys = lax.all_to_all(sent, "seq", split_axis=0, concat_axis=0, tiled=True)

    request_ends = jnp.cumsum(req_blocks)
    first = (request_ends - req_blocks - me * block_count)[:, None]
    last = (request_ends - me * block_count)[:, None]
    part = attend(geo, keep_flags, drop_weight, first, last, queries, cache_keys, cache_values)
    (main,) = pack(geo, keep_flags, drop_weight, cache_values)
    sent = turn(geo, kept_all, main)
    distance = 1
    while distance < peers:
        if distance == peers // 2:
            part, sent = lax.optimization_barrier((part, sent))
        pairs = [(i, i ^ distance) for i in range(peers)]
        if distance == peers // 2:
            part = merge(part, widen(lax.ppermute(narrow(part), "seq", pairs)))
        else:
            part = merge(part, lax.ppermute(part, "seq", pairs))
        distance *= 2
    part, sent = lax.optimization_barrier((part, sent))
    values = lax.all_to_all(sent, "seq", split_axis=0, concat_axis=0, tiled=True)

    counts = jnp.sum(kept_all, axis=1) + block_count
    starts = jnp.cumsum(counts) - counts
    slot = (starts + (me - starts) % peers) // peers
    pick, last, key_tails, value_tails = plan(geo, slot, keys)
    packed_keys = unpack(geo, slot, keys, pick, last, key_tails)
    packed_values = unpack(geo, slot, values, pick, last, value_tails)

    sizes = kept_all.reshape(-1) + 1
    ends = jnp.cumsum(sizes)
    rank = jnp.arange(geo.slots, dtype=jnp.int32) * peers + me
    block = jnp.sum((rank[:, None] >= ends[None, :]).astype(jnp.int32), axis=1)
    folds = rank[:, None] == (ends - 1)[None, :]
    block_bias = jnp.log((BLOCK + 1 - sizes).astype(jnp.float32))
    packed_bias = jnp.sum(jnp.where(folds, block_bias[None, :], 0.0), axis=1).astype(jnp.bfloat16)
    owner = jnp.sum((block[:, None] >= request_ends[None, :]).astype(jnp.int32), axis=1)
    packed_request = jnp.where(rank < ends[-1], owner, -1)

    heads = geo.heads
    peak_score, softmax_total = part[..., HD], part[..., HD + LANES // 2]
    weighted = part[..., :HD]
    score_scale = 1.0 / jnp.sqrt(jnp.float32(HD))
    query_heads = queries.reshape(req_count, heads, HD)
    own_score = (
        jnp.einsum(
            "rhd,rhd->hr",
            query_heads,
            new_keys.reshape(req_count, heads, HD),
            preferred_element_type=jnp.float32,
        )
        * score_scale
    )
    final_peak = jnp.maximum(peak_score, own_score)
    rescale_old = jnp.exp(peak_score - final_peak)
    own_prob = jnp.exp(own_score - final_peak)
    new_value_heads = jnp.transpose(new_values.reshape(req_count, heads, HD), (1, 0, 2)).astype(
        jnp.float32
    )
    softmax_total = softmax_total * rescale_old + own_prob
    weighted = weighted * rescale_old[:, :, None] + own_prob[:, :, None] * new_value_heads
    attention_heads = weighted / softmax_total[:, :, None]
    attention = (
        jnp.transpose(attention_heads, (1, 0, 2))
        .reshape(req_count, heads * HD)
        .astype(jnp.bfloat16)
    )
    partial_output = jnp.dot(attention, out_weight, preferred_element_type=jnp.float32)
    layer_output = lax.psum_scatter(partial_output, "tp", scatter_dimension=0, tiled=True).astype(
        jnp.bfloat16
    )
    return (packed_keys, packed_values, packed_bias, packed_request, layer_output)


def solution(mesh):
    in_specs = (
        P("seq", "tp"),
        P("seq", "tp"),
        P("seq"),
        P("seq"),
        P(),
        P(None, "tp"),
        P(None, "tp"),
        P(None, "tp"),
        P("tp", "seq"),
    )
    out_specs = (P("seq", "tp"), P("seq", "tp"), P("seq"), P("seq"), P("tp", "seq"))
    return jax.shard_map(
        on_device, mesh=mesh, in_specs=in_specs, out_specs=out_specs, check_vma=False
    )
```

```python
import functools

import jax
import jax.numpy as jnp
from jax import lax
from jax.experimental import pallas as pl
from jax.experimental.pallas import tpu as pltpu
from jax.sharding import PartitionSpec as P

HD = 256
BLOCK = 128
LANES = 128
SUB = 16
LEAST_KEPT = BLOCK // 4
MOST_KEPT = BLOCK // 2
LOW = -1e30
VMEM_LIMIT = 56 * 1024 * 1024
TURNS = 4
VMEM_SMALL = 24 * 1024 * 1024


class Geometry:
    def __init__(self, peers, blocks, features):
        self.peers = peers
        self.blocks = blocks
        self.features = features
        self.heads = features // HD
        self.slots = blocks * (MOST_KEPT + 1)
        self.peer_rows = -(-self.slots // peers)
        self.groups = self.peer_rows // SUB
        self.main = self.groups * SUB
        self.chunks = 2 * features // LANES
        self.tail = -(-self.chunks // SUB) * SUB
        self.share = self.chunks // 2 * self.main
        self.group_rows = SUB * peers
        assert self.peer_rows == self.main + 1
        assert self.block_range(self.main * peers, self.slots - 1) == (blocks - 1, blocks)
        self.join = min(peers, max(1, 256 // self.main))
        self.joins = peers // self.join
        window = self.join * self.peer_rows + SUB - 1
        self.window = min(-(-window // SUB) * SUB, self.slots)
        assert self.slots % SUB == 0 and peers % self.join == 0

    def block_range(self, first, last):
        low = max(0, -(-(first - MOST_KEPT) // (MOST_KEPT + 1)))
        high = min(self.blocks - 1, last // (LEAST_KEPT + 1))
        return low, high + 1

    def ranges(self):
        rows = self.group_rows
        return [self.block_range(g * rows, (g + 1) * rows - 1) for g in range(self.groups)]

    def places(self):
        places = [0]
        for low, high in self.ranges():
            places.append(places[-1] + (high - low) * BLOCK)
        return places


def iota(shape, axis):
    return lax.broadcasted_iota(jnp.int32, shape, axis)


def dot(a, b, contract=((1,), (0,))):
    return lax.dot_general(a, b, (contract, ((), ())), preferred_element_type=jnp.float32)


def pack_kernel(geo, tails, keep_ref, weight_ref, cache_ref, *refs):
    step = pl.program_id(0)
    blocks, peers = geo.blocks, geo.peers
    if tails:
        end_refs, (main_ref, tail_ref, pick_ref, scale_ref) = refs[:2], refs[2:]
    else:
        main_ref, pick_ref, scale_ref = refs
    ranges = geo.ranges()
    places = geo.places()

    def flags():
        keep = keep_ref[...].reshape(blocks, BLOCK).astype(jnp.float32)
        weight = weight_ref[...].reshape(blocks, BLOCK).astype(jnp.float32)
        return keep, weight * (1.0 - keep)

    @pl.when(step == 0)
    def _():
        keep, dropped = flags()
        kept = jnp.sum(keep, axis=1, keepdims=True)
        inverse = 1.0 / jnp.sum(dropped, axis=1, keepdims=True)
        earlier = (iota((BLOCK, BLOCK), 0) < iota((BLOCK, BLOCK), 1)).astype(jnp.bfloat16)
        within = dot(keep.astype(jnp.bfloat16), earlier)
        before = (iota((blocks, blocks), 1) < iota((blocks, blocks), 0)).astype(jnp.bfloat16)
        sizes = jnp.broadcast_to(kept + 1.0, (blocks, BLOCK)).astype(jnp.bfloat16)
        base = dot(before, sizes)
        entry = jnp.where(keep > 0.0, base + within, -1.0).astype(jnp.int32)
        fold_entry = (base + kept).astype(jnp.int32)

        def select(index, low, high):
            scale = jnp.ones(index.shape, jnp.float32)
            picks = []
            for b in range(low, high):
                folds = index == fold_entry[b : b + 1, :]
                one = jnp.where(index == entry[b : b + 1, :], 1.0, 0.0)
                picked = jnp.where(folds, dropped[b : b + 1, :], one)
                picks.append(picked.astype(jnp.bfloat16))
                scale = jnp.where(folds, inverse[b : b + 1, :], scale)
            return picks, scale

        row = iota((geo.group_rows, BLOCK), 0)
        for g in range(geo.groups):
            index = (g * SUB + row % SUB) * peers + row // SUB
            picks, scale_ref[g, :, :] = select(index, *ranges[g])
            for i, picked in enumerate(picks):
                at = places[g] + i * BLOCK
                pick_ref[:, at : at + BLOCK] = picked
        if tails:
            index = geo.main * peers + iota((peers, BLOCK), 0)
            (picked,), scale = select(index, blocks - 1, blocks)
            left = []
            for end_ref in end_refs:
                rows = dot(picked, end_ref[...])
                for c in range(geo.chunks // 2):
                    left.append((rows[:, c * LANES : (c + 1) * LANES] * scale).astype(jnp.bfloat16))
            shape = (peers * geo.tail, geo.chunks * peers)
            row, col = iota(shape, 0), iota(shape, 1)
            wanted = row % geo.tail * peers + row // geo.tail
            turn = jnp.where(wanted == col, 1.0, 0.0).astype(jnp.bfloat16)
            rows = dot(turn, jnp.concatenate(left, axis=0)).astype(jnp.bfloat16)
            tail_ref[...] = rows.reshape(peers, geo.tail, LANES)

    for g in range(geo.groups):
        low, high = ranges[g]
        rows = dot(
            pick_ref[:, places[g] : places[g] + (high - low) * BLOCK],
            cache_ref[low * BLOCK : high * BLOCK, :],
        )
        for half in range(HD // LANES):
            chunk = rows[:, half * LANES : (half + 1) * LANES] * scale_ref[g]
            chunk = chunk.astype(jnp.bfloat16).reshape(peers, SUB, LANES)
            at = half * geo.main + g * SUB
            main_ref[:, at : at + SUB, :] = chunk


def attend_kernel(
    geo, keep_ref, weight_ref, first_ref, last_ref, query_ref, key_ref, value_ref,
    part_ref, fold_ref,
):
    step = pl.program_id(0)
    blocks = geo.blocks
    keep = keep_ref[...].reshape(blocks, BLOCK).astype(jnp.float32)
    weight = weight_ref[...].reshape(blocks, BLOCK).astype(jnp.float32)
    dropped = weight * (1.0 - keep)
    inverse = 1.0 / jnp.sum(dropped, axis=1, keepdims=True)

    @pl.when(step == 0)
    def _():
        for b in range(blocks):
            mine = iota((blocks, BLOCK), 0) == b
            fold_ref[:, b * BLOCK : (b + 1) * BLOCK] = jnp.where(
                mine, dropped[b : b + 1, :], 0.0
            ).astype(jnp.bfloat16)

    query = query_ref[...]
    first, last = first_ref[...], last_ref[...]
    requests = query.shape[0]
    score_scale = HD**-0.5
    folded_keys = (dot(fold_ref[...], key_ref[...]) * inverse).astype(jnp.bfloat16)
    folded_values = (dot(fold_ref[...], value_ref[...]) * inverse).astype(jnp.bfloat16)
    ones = jnp.ones((8, BLOCK), jnp.bfloat16)
    kept_lanes = dot(ones, keep.astype(jnp.bfloat16), ((1,), (1,)))[0:1, :]
    bias = jnp.log(BLOCK - kept_lanes).astype(jnp.bfloat16).astype(jnp.float32)
    fold_scores = dot(query, folded_keys, ((1,), (1,))) * score_scale + bias
    block = iota((requests, blocks), 1)
    fold_member = (block >= first) & (block < last)
    fold_scores = jnp.where(fold_member, fold_scores, LOW)
    scores = dot(query, key_ref[...], ((1,), (1,))) * score_scale
    lane_block = iota((requests, blocks * BLOCK), 1) // BLOCK
    kept_rows = jnp.concatenate(
        [jnp.broadcast_to(keep[b : b + 1, :], (requests, BLOCK)) for b in range(blocks)], axis=1
    )
    member = (lane_block >= first) & (lane_block < last) & (kept_rows > 0.0)
    scores = jnp.where(member, scores, LOW)
    peak = jnp.maximum(
        jnp.max(scores, axis=1, keepdims=True), jnp.max(fold_scores, axis=1, keepdims=True)
    )
    probs = jnp.where(member, jnp.exp(scores - peak), 0.0)
    fold_probs = jnp.where(fold_member, jnp.exp(fold_scores - peak), 0.0)
    total = jnp.sum(probs, axis=1, keepdims=True) + jnp.sum(fold_probs, axis=1, keepdims=True)
    mixed = dot(probs.astype(jnp.bfloat16), value_ref[...]) + dot(
        fold_probs.astype(jnp.bfloat16), folded_values
    )
    part_ref[0, :, 0:HD] = mixed
    part_ref[0, :, HD:] = jnp.where(iota((requests, LANES), 1) < LANES // 2, peak, total)


def whole(*shape):
    return pl.BlockSpec(shape, lambda t: (0,) * len(shape))


def pack(geo, keep, weight, cache, ends=()):
    rows = cache.shape[0]
    width = geo.places()[-1]
    end_block = geo.blocks - 1
    out_specs = [pl.BlockSpec((geo.peers, 2 * geo.main, LANES), lambda t: (0, t, 0))]
    out_shape = [jax.ShapeDtypeStruct((geo.peers, geo.share, LANES), jnp.bfloat16)]
    if ends:
        out_specs.append(whole(geo.peers, geo.tail, LANES))
        out_shape.append(jax.ShapeDtypeStruct((geo.peers, geo.tail, LANES), jnp.bfloat16))
    return pl.pallas_call(
        functools.partial(pack_kernel, geo, bool(ends)),
        grid=(geo.heads,),
        in_specs=[whole(rows), whole(rows), pl.BlockSpec((rows, HD), lambda t: (0, t))]
        + [pl.BlockSpec((BLOCK, geo.features), lambda t: (end_block, 0))] * len(ends),
        out_specs=out_specs,
        out_shape=out_shape,
        scratch_shapes=[
            pltpu.VMEM((geo.group_rows, width), jnp.bfloat16),
            pltpu.VMEM((geo.groups, geo.group_rows, BLOCK), jnp.float32),
        ],
        compiler_params=pltpu.CompilerParams(vmem_limit_bytes=VMEM_LIMIT),
        cost_estimate=pl.CostEstimate(
            flops=2 * geo.group_rows * width * geo.features,
            bytes_accessed=3 * rows * geo.features,
            transcendentals=0,
        ),
    )(keep, weight, cache, *ends)


def attend(geo, keep, weight, first, last, queries, cache_keys, cache_values):
    rows = cache_keys.shape[0]
    requests = queries.shape[0]
    return pl.pallas_call(
        functools.partial(attend_kernel, geo),
        grid=(geo.heads,),
        in_specs=[
            whole(rows),
            whole(rows),
            whole(requests, 1),
            whole(requests, 1),
            pl.BlockSpec((requests, HD), lambda t: (0, t)),
            pl.BlockSpec((rows, HD), lambda t: (0, t)),
            pl.BlockSpec((rows, HD), lambda t: (0, t)),
        ],
        out_specs=pl.BlockSpec((1, requests, HD + LANES), lambda t: (t, 0, 0)),
        out_shape=jax.ShapeDtypeStruct((geo.heads, requests, HD + LANES), jnp.float32),
        scratch_shapes=[pltpu.VMEM((geo.blocks, rows), jnp.bfloat16)],
        compiler_params=pltpu.CompilerParams(vmem_limit_bytes=VMEM_LIMIT),
        cost_estimate=pl.CostEstimate(
            flops=8 * rows * requests * geo.features,
            bytes_accessed=2 * rows * geo.features * 2,
            transcendentals=rows * requests * geo.heads,
        ),
    )(keep, weight, first, last, queries, cache_keys, cache_values)


def my_start(kept, me):
    return jnp.sum(jnp.where(iota(kept.shape, 0) < me, kept + 1, 0))


def turn_kernel(geo, kept_ref, *refs):
    main_ref, tail_refs = refs[0], refs[1:-7]
    sent_ref, counts_ref, held_ref, counts_sem, main_sems, tail_sem, out_sems = refs[-7:]
    me = lax.axis_index("seq")
    peers, share = geo.peers, geo.share
    counts = pltpu.make_async_copy(kept_ref, counts_ref, counts_sem)
    counts.start()
    tails = [
        pltpu.make_async_copy(ref, held_ref.at[:, share : share + geo.tail], tail_sem)
        for ref in tail_refs
    ]
    for copy in tails:
        copy.start()
    size = peers // TURNS
    mains = []
    for i in range(TURNS):
        some = slice(i * size, (i + 1) * size)
        mains.append(
            pltpu.make_async_copy(main_ref.at[some], held_ref.at[some, 0:share], main_sems.at[i])
        )
        mains[i].start()
    counts.wait()
    start = my_start(counts_ref[...], me)
    for copy in tails:
        copy.wait()
    departures = []
    for p in range(peers):
        if p % size == 0:
            mains[p // size].wait()
        device = lax.rem(start + p, peers)
        departures.append(
            pltpu.make_async_copy(held_ref.at[p], sent_ref.at[device], out_sems.at[p])
        )
        departures[p].start()
    for copy in departures:
        copy.wait()


def turn(geo, kept, main, tail=None):
    tails = [] if tail is None else [tail]
    shape = (geo.peers, geo.share + len(tails) * geo.tail, LANES)
    size = geo.peers * geo.share * LANES
    return pl.pallas_call(
        functools.partial(turn_kernel, geo),
        in_specs=[pl.BlockSpec(memory_space=pl.ANY)] * (2 + len(tails)),
        out_specs=pl.BlockSpec(memory_space=pl.ANY),
        out_shape=jax.ShapeDtypeStruct(shape, jnp.bfloat16),
        scratch_shapes=[
            pltpu.VMEM(kept.shape, jnp.int32),
            pltpu.VMEM(shape, jnp.bfloat16),
            pltpu.SemaphoreType.DMA,
            pltpu.SemaphoreType.DMA((TURNS,)),
            pltpu.SemaphoreType.DMA,
            pltpu.SemaphoreType.DMA((geo.peers,)),
        ],
        compiler_params=pltpu.CompilerParams(vmem_limit_bytes=VMEM_LIMIT),
        cost_estimate=pl.CostEstimate(flops=0, bytes_accessed=4 * size, transcendentals=0),
    )(kept, main, *tails)


def low_slots(geo, slot_ref):
    lows = []
    for q in range(geo.joins):
        low = jnp.minimum(slot_ref[q * geo.join] // SUB * SUB, geo.slots - geo.window)
        lows.append(pl.multiple_of(low, SUB))
    return lows


def plan_kernel(geo, slot_ref, tail_ref, pick_ref, last_ref, keys_ref, values_ref):
    peers, main = geo.peers, geo.main
    width = geo.join * main
    lows = low_slots(geo, slot_ref)
    for q in range(geo.joins):
        lane = iota((1, width), 1)
        target = lane % main
        last = jnp.full((1, peers), -1, jnp.int32)
        for j in range(geo.join):
            at = slot_ref[q * geo.join + j] - lows[q]
            target = target + jnp.where(lane // main == j, at, 0)
            last = jnp.where(iota((1, peers), 1) == q * geo.join + j, at + main, last)
        picked = jnp.where(iota((geo.window, width), 0) == target, 1.0, 0.0)
        pick_ref[q, :, :] = picked.astype(jnp.bfloat16)
        picked = jnp.where(iota((geo.window, peers), 0) == last, 1.0, 0.0)
        last_ref[q, :, :] = picked.astype(jnp.bfloat16)
    tails = tail_ref[...].reshape(peers * geo.tail, LANES)
    share = geo.chunks // 2
    for part, out_ref in enumerate((keys_ref, values_ref)):
        shape = (share * peers, peers * geo.tail)
        row, col = iota(shape, 0), iota(shape, 1)
        wanted = row % peers * geo.tail + row // peers + part * share
        back = jnp.where(wanted == col, 1.0, 0.0).astype(jnp.bfloat16)
        rows = dot(back, tails).astype(jnp.bfloat16)
        for c in range(share):
            at = c * LANES
            out_ref[:, at : at + LANES] = rows[c * peers : (c + 1) * peers, :]


def plan(geo, slot, slabs):
    tail_block = geo.share // geo.tail
    picks = [(geo.joins, geo.window, n) for n in (geo.join * geo.main, geo.peers)]
    shapes = picks + [(geo.peers, geo.features)] * 2
    return pl.pallas_call(
        functools.partial(plan_kernel, geo),
        grid=(1,),
        in_specs=[
            pl.BlockSpec(memory_space=pltpu.SMEM),
            pl.BlockSpec((geo.peers, geo.tail, LANES), lambda t: (0, tail_block, 0)),
        ],
        out_specs=[whole(*shape) for shape in shapes],
        out_shape=[jax.ShapeDtypeStruct(shape, jnp.bfloat16) for shape in shapes],
        compiler_params=pltpu.CompilerParams(vmem_limit_bytes=VMEM_SMALL),
    )(slot, slabs)


def unpack_kernel(geo, slot_ref, slab_ref, pick_ref, last_ref, tail_ref, out_ref):
    main = geo.main
    width = geo.join * main
    lows = low_slots(geo, slot_ref)
    out_ref[...] = jnp.zeros_like(out_ref)
    for q in range(geo.joins):
        sources = slice(q * geo.join, (q + 1) * geo.join)
        rows = [
            slab_ref[sources, c * main : (c + 1) * main, :].reshape(width, LANES)
            for c in range(out_ref.shape[1] // LANES)
        ]
        placed = dot(pick_ref[q], jnp.concatenate(rows, axis=1))
        placed = placed + dot(last_ref[q], tail_ref[...])
        out_ref[pl.ds(lows[q], geo.window), :] += placed.astype(jnp.bfloat16)


def unpack(geo, slot, slabs, pick, last, tail):
    tile = HD * (2 if geo.heads % 2 == 0 else 1)
    tile_rows = tile // LANES * geo.main
    return pl.pallas_call(
        functools.partial(unpack_kernel, geo),
        grid=(geo.features // tile,),
        in_specs=[
            pl.BlockSpec(memory_space=pltpu.SMEM),
            pl.BlockSpec((geo.peers, tile_rows, LANES), lambda t: (0, t, 0)),
            whole(*pick.shape),
            whole(*last.shape),
            pl.BlockSpec((geo.peers, tile), lambda t: (0, t)),
        ],
        out_specs=pl.BlockSpec((geo.slots, tile), lambda t: (0, t)),
        out_shape=jax.ShapeDtypeStruct((geo.slots, geo.features), jnp.bfloat16),
        compiler_params=pltpu.CompilerParams(vmem_limit_bytes=VMEM_SMALL),
        cost_estimate=pl.CostEstimate(
            flops=2 * geo.joins * geo.window * 256 * geo.features,
            bytes_accessed=4 * geo.peers * geo.share * LANES,
            transcendentals=0,
        ),
    )(slot, slabs, pick, last, tail)


def merge(one, two):
    half = HD + LANES // 2
    peak_one, peak_two = one[..., HD : HD + 1], two[..., HD : HD + 1]
    peak = jnp.maximum(peak_one, peak_two)
    rescale_one, rescale_two = jnp.exp(peak_one - peak), jnp.exp(peak_two - peak)
    mixed = one * rescale_one + two * rescale_two
    lane = lax.broadcasted_iota(jnp.int32, one.shape, len(one.shape) - 1)
    return jnp.where((lane >= HD) & (lane < half), peak, mixed)


def narrow(part):
    peak, total = HD, HD + LANES // 2
    lane = lax.broadcasted_iota(jnp.int32, part.shape, len(part.shape) - 1)
    high = lax.reduce_precision(part, 8, 7)
    rest = part - high
    middle = lax.reduce_precision(rest, 8, 7)
    low = lax.reduce_precision(rest - middle, 8, 7)
    second = ((lane >= peak + 16) & (lane < peak + 32)) | (lane >= total + 16)
    third = (lane >= peak + 32) & (lane < total)
    return jnp.where(second, middle, jnp.where(third, low, high)).astype(jnp.bfloat16)


def widen(part):
    peak, total = HD, HD + LANES // 2
    part = part.astype(jnp.float32)
    lane = lax.broadcasted_iota(jnp.int32, part.shape, len(part.shape) - 1)
    peaks = part[..., peak : peak + 1] + part[..., peak + 16 : peak + 17]
    peaks = peaks + part[..., peak + 32 : peak + 33]
    totals = part[..., total : total + 1] + part[..., total + 16 : total + 17]
    return jnp.where(lane >= total, totals, jnp.where(lane >= peak, peaks, part))


def on_device(
    cache_keys, cache_values, keep_flags, drop_weight, req_blocks, queries, new_keys, new_values,
    out_weight,
):
    peers = lax.axis_size("seq")
    me = lax.axis_index("seq")
    row_count, features = cache_keys.shape
    block_count = row_count // BLOCK
    geo = Geometry(peers, block_count, features)
    req_count = queries.shape[0]
    kept_count = jnp.sum(keep_flags.reshape(block_count, BLOCK), axis=1)
    kept_all = lax.all_to_all(
        jnp.broadcast_to(kept_count[None, :], (peers, block_count)),
        "seq", split_axis=0, concat_axis=0, tiled=True,
    )

    main, tail = pack(geo, keep_flags, drop_weight, cache_keys, (cache_keys, cache_values))
    sent = turn(geo, kept_all, main, tail)
    tied = (sent, keep_flags, drop_weight, kept_all, req_blocks)
    sent, keep_flags, drop_weight, kept_all, req_blocks = lax.optimization_barrier(tied)
    keys = lax.all_to_all(sent, "seq", split_axis=0, concat_axis=0, tiled=True)

    request_ends = jnp.cumsum(req_blocks)
    first = (request_ends - req_blocks - me * block_count)[:, None]
    last = (request_ends - me * block_count)[:, None]
    part = attend(geo, keep_flags, drop_weight, first, last, queries, cache_keys, cache_values)
    (main,) = pack(geo, keep_flags, drop_weight, cache_values)
    sent = turn(geo, kept_all, main)
    part = part.reshape(-1, part.shape[-1])
    distance = 1
    while distance < peers // 2:
        pairs = [(i, i ^ distance) for i in range(peers)]
        part = merge(part, lax.ppermute(part, "seq", pairs))
        distance *= 2
    part, sent = lax.optimization_barrier((part, sent))
    other = lax.ppermute(narrow(part), "seq", [(i, i ^ distance) for i in range(peers)])
    other, sent = lax.optimization_barrier((other, sent))
    part = merge(part, widen(other)).reshape(geo.heads, -1, part.shape[-1])
    values = lax.all_to_all(sent, "seq", split_axis=0, concat_axis=0, tiled=True)

    counts = jnp.sum(kept_all, axis=1) + block_count
    starts = jnp.cumsum(counts) - counts
    slot = (starts + (me - starts) % peers) // peers
    pick, last, key_tails, value_tails = plan(geo, slot, keys)
    packed_keys = unpack(geo, slot, keys, pick, last, key_tails)
    packed_values = unpack(geo, slot, values, pick, last, value_tails)

    sizes = kept_all.reshape(-1) + 1
    ends = jnp.cumsum(sizes)
    rank = jnp.arange(geo.slots, dtype=jnp.int32) * peers + me
    block = jnp.sum((rank[:, None] >= ends[None, :]).astype(jnp.int32), axis=1)
    folds = rank[:, None] == (ends - 1)[None, :]
    block_bias = jnp.log((BLOCK + 1 - sizes).astype(jnp.float32))
    packed_bias = jnp.sum(jnp.where(folds, block_bias[None, :], 0.0), axis=1).astype(jnp.bfloat16)
    owner = jnp.sum((block[:, None] >= request_ends[None, :]).astype(jnp.int32), axis=1)
    packed_request = jnp.where(rank < ends[-1], owner, -1)

    heads = geo.heads
    peak_score, softmax_total = part[..., HD], part[..., HD + LANES // 2]
    weighted = part[..., :HD]
    score_scale = 1.0 / jnp.sqrt(jnp.float32(HD))
    query_heads = queries.reshape(req_count, heads, HD)
    own_score = (
        jnp.einsum(
            "rhd,rhd->hr",
            query_heads,
            new_keys.reshape(req_count, heads, HD),
            preferred_element_type=jnp.float32,
        )
        * score_scale
    )
    final_peak = jnp.maximum(peak_score, own_score)
    rescale_old = jnp.exp(peak_score - final_peak)
    own_prob = jnp.exp(own_score - final_peak)
    new_value_heads = jnp.transpose(new_values.reshape(req_count, heads, HD), (1, 0, 2)).astype(
        jnp.float32
    )
    softmax_total = softmax_total * rescale_old + own_prob
    weighted = weighted * rescale_old[:, :, None] + own_prob[:, :, None] * new_value_heads
    attention_heads = weighted / softmax_total[:, :, None]
    attention = (
        jnp.transpose(attention_heads, (1, 0, 2))
        .reshape(req_count, heads * HD)
        .astype(jnp.bfloat16)
    )
    partial_output = jnp.dot(attention, out_weight, preferred_element_type=jnp.float32)
    layer_output = lax.psum_scatter(partial_output, "tp", scatter_dimension=0, tiled=True).astype(
        jnp.bfloat16
    )
    return (packed_keys, packed_values, packed_bias, packed_request, layer_output)


def solution(mesh):
    in_specs = (
        P("seq", "tp"),
        P("seq", "tp"),
        P("seq"),
        P("seq"),
        P(),
        P(None, "tp"),
        P(None, "tp"),
        P(None, "tp"),
        P("tp", "seq"),
    )
    out_specs = (P("seq", "tp"), P("seq", "tp"), P("seq"), P("seq"), P("tp", "seq"))
    return jax.shard_map(
        on_device, mesh=mesh, in_specs=in_specs, out_specs=out_specs, check_vma=False
    )
```

```python
import functools

import jax
import jax.numpy as jnp
from jax import lax
from jax.experimental import pallas as pl
from jax.experimental.pallas import tpu as pltpu
from jax.sharding import PartitionSpec as P

HD = 256
BLOCK = 128
LANES = 128
SUB = 16
LEAST_KEPT = BLOCK // 4
MOST_KEPT = BLOCK // 2
LOW = -1e30
VMEM_LIMIT = 56 * 1024 * 1024
TURNS = 4
VMEM_SMALL = 24 * 1024 * 1024


class Geometry:
    def __init__(self, peers, blocks, features):
        self.peers = peers
        self.blocks = blocks
        self.features = features
        self.heads = features // HD
        self.slots = blocks * (MOST_KEPT + 1)
        self.peer_rows = -(-self.slots // peers)
        self.groups = self.peer_rows // SUB
        self.main = self.groups * SUB
        self.chunks = 2 * features // LANES
        self.tail = -(-self.chunks // SUB) * SUB
        self.share = self.chunks // 2 * self.main
        self.group_rows = SUB * peers
        assert self.peer_rows == self.main + 1
        assert self.block_range(self.main * peers, self.slots - 1) == (blocks - 1, blocks)
        self.join = min(peers, max(1, 256 // self.main))
        self.joins = peers // self.join
        window = self.join * self.peer_rows + SUB - 1
        self.window = min(-(-window // SUB) * SUB, self.slots)
        assert self.slots % SUB == 0 and peers % self.join == 0

    def block_range(self, first, last):
        low = max(0, -(-(first - MOST_KEPT) // (MOST_KEPT + 1)))
        high = min(self.blocks - 1, last // (LEAST_KEPT + 1))
        return low, high + 1

    def ranges(self):
        rows = self.group_rows
        return [self.block_range(g * rows, (g + 1) * rows - 1) for g in range(self.groups)]

    def places(self):
        places = [0]
        for low, high in self.ranges():
            places.append(places[-1] + (high - low) * BLOCK)
        return places


def iota(shape, axis):
    return lax.broadcasted_iota(jnp.int32, shape, axis)


def dot(a, b, contract=((1,), (0,))):
    return lax.dot_general(a, b, (contract, ((), ())), preferred_element_type=jnp.float32)


def pack_kernel(geo, tails, keep_ref, weight_ref, cache_ref, *refs):
    step = pl.program_id(0)
    blocks, peers = geo.blocks, geo.peers
    if tails:
        end_refs, (main_ref, tail_ref, pick_ref, scale_ref) = refs[:2], refs[2:]
    else:
        main_ref, pick_ref, scale_ref = refs
    ranges = geo.ranges()
    places = geo.places()

    def flags():
        keep = keep_ref[...].reshape(blocks, BLOCK).astype(jnp.float32)
        weight = weight_ref[...].reshape(blocks, BLOCK).astype(jnp.float32)
        return keep, weight * (1.0 - keep)

    @pl.when(step == 0)
    def _():
        keep, dropped = flags()
        kept = jnp.sum(keep, axis=1, keepdims=True)
        inverse = 1.0 / jnp.sum(dropped, axis=1, keepdims=True)
        earlier = (iota((BLOCK, BLOCK), 0) < iota((BLOCK, BLOCK), 1)).astype(jnp.bfloat16)
        within = dot(keep.astype(jnp.bfloat16), earlier)
        before = (iota((blocks, blocks), 1) < iota((blocks, blocks), 0)).astype(jnp.bfloat16)
        sizes = jnp.broadcast_to(kept + 1.0, (blocks, BLOCK)).astype(jnp.bfloat16)
        base = dot(before, sizes)
        entry = jnp.where(keep > 0.0, base + within, -1.0).astype(jnp.int32)
        fold_entry = (base + kept).astype(jnp.int32)

        def select(index, low, high):
            scale = jnp.ones(index.shape, jnp.float32)
            picks = []
            for b in range(low, high):
                folds = index == fold_entry[b : b + 1, :]
                one = jnp.where(index == entry[b : b + 1, :], 1.0, 0.0)
                picked = jnp.where(folds, dropped[b : b + 1, :], one)
                picks.append(picked.astype(jnp.bfloat16))
                scale = jnp.where(folds, inverse[b : b + 1, :], scale)
            return picks, scale

        row = iota((geo.group_rows, BLOCK), 0)
        for g in range(geo.groups):
            index = (g * SUB + row % SUB) * peers + row // SUB
            picks, scale_ref[g, :, :] = select(index, *ranges[g])
            for i, picked in enumerate(picks):
                at = places[g] + i * BLOCK
                pick_ref[:, at : at + BLOCK] = picked
        if tails:
            index = geo.main * peers + iota((peers, BLOCK), 0)
            (picked,), scale = select(index, blocks - 1, blocks)
            left = []
            for end_ref in end_refs:
                rows = dot(picked, end_ref[...])
                for c in range(geo.chunks // 2):
                    left.append((rows[:, c * LANES : (c + 1) * LANES] * scale).astype(jnp.bfloat16))
            shape = (peers * geo.tail, geo.chunks * peers)
            row, col = iota(shape, 0), iota(shape, 1)
            wanted = row % geo.tail * peers + row // geo.tail
            turn = jnp.where(wanted == col, 1.0, 0.0).astype(jnp.bfloat16)
            rows = dot(turn, jnp.concatenate(left, axis=0)).astype(jnp.bfloat16)
            tail_ref[...] = rows.reshape(peers, geo.tail, LANES)

    for g in range(geo.groups):
        low, high = ranges[g]
        rows = dot(
            pick_ref[:, places[g] : places[g] + (high - low) * BLOCK],
            cache_ref[low * BLOCK : high * BLOCK, :],
        )
        for half in range(HD // LANES):
            chunk = rows[:, half * LANES : (half + 1) * LANES] * scale_ref[g]
            chunk = chunk.astype(jnp.bfloat16).reshape(peers, SUB, LANES)
            at = half * geo.main + g * SUB
            main_ref[:, at : at + SUB, :] = chunk


def attend_kernel(
    geo, keep_ref, weight_ref, first_ref, last_ref, query_ref, key_ref, value_ref,
    part_ref, fold_ref,
):
    step = pl.program_id(0)
    blocks = geo.blocks
    keep = keep_ref[...].reshape(blocks, BLOCK).astype(jnp.float32)
    weight = weight_ref[...].reshape(blocks, BLOCK).astype(jnp.float32)
    dropped = weight * (1.0 - keep)
    inverse = 1.0 / jnp.sum(dropped, axis=1, keepdims=True)

    @pl.when(step == 0)
    def _():
        for b in range(blocks):
            mine = iota((blocks, BLOCK), 0) == b
            fold_ref[:, b * BLOCK : (b + 1) * BLOCK] = jnp.where(
                mine, dropped[b : b + 1, :], 0.0
            ).astype(jnp.bfloat16)

    query = query_ref[...]
    first, last = first_ref[...], last_ref[...]
    requests = query.shape[0]
    score_scale = HD**-0.5
    folded_keys = (dot(fold_ref[...], key_ref[...]) * inverse).astype(jnp.bfloat16)
    folded_values = (dot(fold_ref[...], value_ref[...]) * inverse).astype(jnp.bfloat16)
    ones = jnp.ones((8, BLOCK), jnp.bfloat16)
    kept_lanes = dot(ones, keep.astype(jnp.bfloat16), ((1,), (1,)))[0:1, :]
    bias = jnp.log(BLOCK - kept_lanes).astype(jnp.bfloat16).astype(jnp.float32)
    fold_scores = dot(query, folded_keys, ((1,), (1,))) * score_scale + bias
    block = iota((requests, blocks), 1)
    fold_member = (block >= first) & (block < last)
    fold_scores = jnp.where(fold_member, fold_scores, LOW)
    scores = dot(query, key_ref[...], ((1,), (1,))) * score_scale
    lane_block = iota((requests, blocks * BLOCK), 1) // BLOCK
    kept_rows = jnp.concatenate(
        [jnp.broadcast_to(keep[b : b + 1, :], (requests, BLOCK)) for b in range(blocks)], axis=1
    )
    member = (lane_block >= first) & (lane_block < last) & (kept_rows > 0.0)
    scores = jnp.where(member, scores, LOW)
    peak = jnp.maximum(
        jnp.max(scores, axis=1, keepdims=True), jnp.max(fold_scores, axis=1, keepdims=True)
    )
    probs = jnp.where(member, jnp.exp(scores - peak), 0.0)
    fold_probs = jnp.where(fold_member, jnp.exp(fold_scores - peak), 0.0)
    total = jnp.sum(probs, axis=1, keepdims=True) + jnp.sum(fold_probs, axis=1, keepdims=True)
    mixed = dot(probs.astype(jnp.bfloat16), value_ref[...]) + dot(
        fold_probs.astype(jnp.bfloat16), folded_values
    )
    part_ref[0, :, 0:HD] = mixed
    part_ref[0, :, HD:] = jnp.where(iota((requests, LANES), 1) < LANES // 2, peak, total)


def whole(*shape):
    return pl.BlockSpec(shape, lambda t: (0,) * len(shape))


def pack(geo, keep, weight, cache, ends=()):
    rows = cache.shape[0]
    width = geo.places()[-1]
    end_block = geo.blocks - 1
    out_specs = [pl.BlockSpec((geo.peers, 2 * geo.main, LANES), lambda t: (0, t, 0))]
    out_shape = [jax.ShapeDtypeStruct((geo.peers, geo.share, LANES), jnp.bfloat16)]
    if ends:
        out_specs.append(whole(geo.peers, geo.tail, LANES))
        out_shape.append(jax.ShapeDtypeStruct((geo.peers, geo.tail, LANES), jnp.bfloat16))
    return pl.pallas_call(
        functools.partial(pack_kernel, geo, bool(ends)),
        grid=(geo.heads,),
        in_specs=[whole(rows), whole(rows), pl.BlockSpec((rows, HD), lambda t: (0, t))]
        + [pl.BlockSpec((BLOCK, geo.features), lambda t: (end_block, 0))] * len(ends),
        out_specs=out_specs,
        out_shape=out_shape,
        scratch_shapes=[
            pltpu.VMEM((geo.group_rows, width), jnp.bfloat16),
            pltpu.VMEM((geo.groups, geo.group_rows, BLOCK), jnp.float32),
        ],
        compiler_params=pltpu.CompilerParams(vmem_limit_bytes=VMEM_LIMIT),
        cost_estimate=pl.CostEstimate(
            flops=2 * geo.group_rows * width * geo.features,
            bytes_accessed=3 * rows * geo.features,
            transcendentals=0,
        ),
    )(keep, weight, cache, *ends)


def attend(geo, keep, weight, first, last, queries, cache_keys, cache_values):
    rows = cache_keys.shape[0]
    requests = queries.shape[0]
    return pl.pallas_call(
        functools.partial(attend_kernel, geo),
        grid=(geo.heads,),
        in_specs=[
            whole(rows),
            whole(rows),
            whole(requests, 1),
            whole(requests, 1),
            pl.BlockSpec((requests, HD), lambda t: (0, t)),
            pl.BlockSpec((rows, HD), lambda t: (0, t)),
            pl.BlockSpec((rows, HD), lambda t: (0, t)),
        ],
        out_specs=pl.BlockSpec((1, requests, HD + LANES), lambda t: (t, 0, 0)),
        out_shape=jax.ShapeDtypeStruct((geo.heads, requests, HD + LANES), jnp.float32),
        scratch_shapes=[pltpu.VMEM((geo.blocks, rows), jnp.bfloat16)],
        compiler_params=pltpu.CompilerParams(vmem_limit_bytes=VMEM_LIMIT),
        cost_estimate=pl.CostEstimate(
            flops=8 * rows * requests * geo.features,
            bytes_accessed=2 * rows * geo.features * 2,
            transcendentals=rows * requests * geo.heads,
        ),
    )(keep, weight, first, last, queries, cache_keys, cache_values)


def my_start(kept, me):
    return jnp.sum(jnp.where(iota(kept.shape, 0) < me, kept + 1, 0))


def turn_kernel(geo, kept_ref, *refs):
    main_ref, tail_refs = refs[0], refs[1:-7]
    sent_ref, counts_ref, held_ref, counts_sem, main_sems, tail_sem, out_sems = refs[-7:]
    me = lax.axis_index("seq")
    peers, share = geo.peers, geo.share
    counts = pltpu.make_async_copy(kept_ref, counts_ref, counts_sem)
    counts.start()
    tails = [
        pltpu.make_async_copy(ref, held_ref.at[:, share : share + geo.tail], tail_sem)
        for ref in tail_refs
    ]
    for copy in tails:
        copy.start()
    size = peers // TURNS
    mains = []
    for i in range(TURNS):
        some = slice(i * size, (i + 1) * size)
        mains.append(
            pltpu.make_async_copy(main_ref.at[some], held_ref.at[some, 0:share], main_sems.at[i])
        )
        mains[i].start()
    counts.wait()
    start = my_start(counts_ref[...], me)
    for copy in tails:
        copy.wait()
    departures = []
    for p in range(peers):
        if p % size == 0:
            mains[p // size].wait()
        device = lax.rem(start + p, peers)
        departures.append(
            pltpu.make_async_copy(held_ref.at[p], sent_ref.at[device], out_sems.at[p])
        )
        departures[p].start()
    for copy in departures:
        copy.wait()


def turn(geo, kept, main, tail=None):
    tails = [] if tail is None else [tail]
    shape = (geo.peers, geo.share + len(tails) * geo.tail, LANES)
    size = geo.peers * geo.share * LANES
    return pl.pallas_call(
        functools.partial(turn_kernel, geo),
        in_specs=[pl.BlockSpec(memory_space=pl.ANY)] * (2 + len(tails)),
        out_specs=pl.BlockSpec(memory_space=pl.ANY),
        out_shape=jax.ShapeDtypeStruct(shape, jnp.bfloat16),
        scratch_shapes=[
            pltpu.VMEM(kept.shape, jnp.int32),
            pltpu.VMEM(shape, jnp.bfloat16),
            pltpu.SemaphoreType.DMA,
            pltpu.SemaphoreType.DMA((TURNS,)),
            pltpu.SemaphoreType.DMA,
            pltpu.SemaphoreType.DMA((geo.peers,)),
        ],
        compiler_params=pltpu.CompilerParams(vmem_limit_bytes=VMEM_LIMIT),
        cost_estimate=pl.CostEstimate(flops=0, bytes_accessed=4 * size, transcendentals=0),
    )(kept, main, *tails)


def low_slots(geo, slot_ref):
    lows = []
    for q in range(geo.joins):
        low = jnp.minimum(slot_ref[q * geo.join] // SUB * SUB, geo.slots - geo.window)
        lows.append(pl.multiple_of(low, SUB))
    return lows


def plan_kernel(geo, slot_ref, tail_ref, pick_ref, last_ref, keys_ref, values_ref):
    peers, main = geo.peers, geo.main
    width = geo.join * main
    lows = low_slots(geo, slot_ref)
    for q in range(geo.joins):
        lane = iota((1, width), 1)
        target = lane % main
        last = jnp.full((1, peers), -1, jnp.int32)
        for j in range(geo.join):
            at = slot_ref[q * geo.join + j] - lows[q]
            target = target + jnp.where(lane // main == j, at, 0)
            last = jnp.where(iota((1, peers), 1) == q * geo.join + j, at + main, last)
        picked = jnp.where(iota((geo.window, width), 0) == target, 1.0, 0.0)
        pick_ref[q, :, :] = picked.astype(jnp.bfloat16)
        picked = jnp.where(iota((geo.window, peers), 0) == last, 1.0, 0.0)
        last_ref[q, :, :] = picked.astype(jnp.bfloat16)
    tails = tail_ref[...].reshape(peers * geo.tail, LANES)
    share = geo.chunks // 2
    for part, out_ref in enumerate((keys_ref, values_ref)):
        shape = (share * peers, peers * geo.tail)
        row, col = iota(shape, 0), iota(shape, 1)
        wanted = row % peers * geo.tail + row // peers + part * share
        back = jnp.where(wanted == col, 1.0, 0.0).astype(jnp.bfloat16)
        rows = dot(back, tails).astype(jnp.bfloat16)
        for c in range(share):
            at = c * LANES
            out_ref[:, at : at + LANES] = rows[c * peers : (c + 1) * peers, :]


def plan(geo, slot, slabs):
    tail_block = geo.share // geo.tail
    picks = [(geo.joins, geo.window, n) for n in (geo.join * geo.main, geo.peers)]
    shapes = picks + [(geo.peers, geo.features)] * 2
    return pl.pallas_call(
        functools.partial(plan_kernel, geo),
        grid=(1,),
        in_specs=[
            pl.BlockSpec(memory_space=pltpu.SMEM),
            pl.BlockSpec((geo.peers, geo.tail, LANES), lambda t: (0, tail_block, 0)),
        ],
        out_specs=[whole(*shape) for shape in shapes],
        out_shape=[jax.ShapeDtypeStruct(shape, jnp.bfloat16) for shape in shapes],
        compiler_params=pltpu.CompilerParams(vmem_limit_bytes=VMEM_SMALL),
    )(slot, slabs)


def unpack_kernel(geo, slot_ref, slab_ref, pick_ref, last_ref, tail_ref, out_ref):
    main = geo.main
    width = geo.join * main
    lows = low_slots(geo, slot_ref)
    out_ref[...] = jnp.zeros_like(out_ref)
    for q in range(geo.joins):
        sources = slice(q * geo.join, (q + 1) * geo.join)
        rows = [
            slab_ref[sources, c * main : (c + 1) * main, :].reshape(width, LANES)
            for c in range(out_ref.shape[1] // LANES)
        ]
        placed = dot(pick_ref[q], jnp.concatenate(rows, axis=1))
        placed = placed + dot(last_ref[q], tail_ref[...])
        out_ref[pl.ds(lows[q], geo.window), :] += placed.astype(jnp.bfloat16)


def unpack(geo, slot, slabs, pick, last, tail):
    tile = HD * (2 if geo.heads % 2 == 0 else 1)
    tile_rows = tile // LANES * geo.main
    return pl.pallas_call(
        functools.partial(unpack_kernel, geo),
        grid=(geo.features // tile,),
        in_specs=[
            pl.BlockSpec(memory_space=pltpu.SMEM),
            pl.BlockSpec((geo.peers, tile_rows, LANES), lambda t: (0, t, 0)),
            whole(*pick.shape),
            whole(*last.shape),
            pl.BlockSpec((geo.peers, tile), lambda t: (0, t)),
        ],
        out_specs=pl.BlockSpec((geo.slots, tile), lambda t: (0, t)),
        out_shape=jax.ShapeDtypeStruct((geo.slots, geo.features), jnp.bfloat16),
        compiler_params=pltpu.CompilerParams(vmem_limit_bytes=VMEM_SMALL),
        cost_estimate=pl.CostEstimate(
            flops=2 * geo.joins * geo.window * 256 * geo.features,
            bytes_accessed=4 * geo.peers * geo.share * LANES,
            transcendentals=0,
        ),
    )(slot, slabs, pick, last, tail)


def merge(one, two):
    half = HD + LANES // 2
    peak_one, peak_two = one[..., HD : HD + 1], two[..., HD : HD + 1]
    peak = jnp.maximum(peak_one, peak_two)
    rescale_one, rescale_two = jnp.exp(peak_one - peak), jnp.exp(peak_two - peak)
    mixed = one * rescale_one + two * rescale_two
    lane = lax.broadcasted_iota(jnp.int32, one.shape, len(one.shape) - 1)
    return jnp.where((lane >= HD) & (lane < half), peak, mixed)


def narrow(part):
    peak, total = HD, HD + LANES // 2
    lane = lax.broadcasted_iota(jnp.int32, part.shape, len(part.shape) - 1)
    high = lax.reduce_precision(part, 8, 7)
    rest = part - high
    middle = lax.reduce_precision(rest, 8, 7)
    low = lax.reduce_precision(rest - middle, 8, 7)
    second = ((lane >= peak + 16) & (lane < peak + 32)) | (lane >= total + 16)
    third = (lane >= peak + 32) & (lane < total)
    return jnp.where(second, middle, jnp.where(third, low, high)).astype(jnp.bfloat16)


def widen(part):
    peak, total = HD, HD + LANES // 2
    part = part.astype(jnp.float32)
    lane = lax.broadcasted_iota(jnp.int32, part.shape, len(part.shape) - 1)
    peaks = part[..., peak : peak + 1] + part[..., peak + 16 : peak + 17]
    peaks = peaks + part[..., peak + 32 : peak + 33]
    totals = part[..., total : total + 1] + part[..., total + 16 : total + 17]
    return jnp.where(lane >= total, totals, jnp.where(lane >= peak, peaks, part))


def on_device(
    cache_keys, cache_values, keep_flags, drop_weight, req_blocks, queries, new_keys, new_values,
    out_weight,
):
    peers = lax.axis_size("seq")
    me = lax.axis_index("seq")
    row_count, features = cache_keys.shape
    block_count = row_count // BLOCK
    geo = Geometry(peers, block_count, features)
    req_count = queries.shape[0]
    kept_count = jnp.sum(keep_flags.reshape(block_count, BLOCK), axis=1)
    kept_all = lax.all_to_all(
        jnp.broadcast_to(kept_count[None, :], (peers, block_count)),
        "seq", split_axis=0, concat_axis=0, tiled=True,
    )

    main, tail = pack(geo, keep_flags, drop_weight, cache_keys, (cache_keys, cache_values))
    sent = turn(geo, kept_all, main, tail)
    tied = (sent, keep_flags, drop_weight, kept_all, req_blocks)
    sent, keep_flags, drop_weight, kept_all, req_blocks = lax.optimization_barrier(tied)
    keys = lax.all_to_all(sent, "seq", split_axis=0, concat_axis=0, tiled=True)

    request_ends = jnp.cumsum(req_blocks)
    first = (request_ends - req_blocks - me * block_count)[:, None]
    last = (request_ends - me * block_count)[:, None]
    part = attend(geo, keep_flags, drop_weight, first, last, queries, cache_keys, cache_values)
    (main,) = pack(geo, keep_flags, drop_weight, cache_values)
    sent = turn(geo, kept_all, main)
    part = part.reshape(-1, part.shape[-1])
    distance = 1
    while distance < peers // 2:
        pairs = [(i, i ^ distance) for i in range(peers)]
        part = merge(part, lax.ppermute(part, "seq", pairs))
        distance *= 2
    part, sent = lax.optimization_barrier((part, sent))
    quarter = part.shape[0] // 4
    part = lax.dynamic_slice_in_dim(part, me % 4 * quarter, quarter, 0)
    other = lax.ppermute(narrow(part), "seq", [(i, i ^ distance) for i in range(peers)])
    other, sent = lax.optimization_barrier((other, sent))
    part = merge(part, widen(other))
    for distance in (1, 2):
        other = lax.ppermute(part, "seq", [(i, i ^ distance) for i in range(peers)])
        is_low = me & distance == 0
        part = jnp.concatenate(
            [jnp.where(is_low, part, other), jnp.where(is_low, other, part)], axis=0
        )
    part = part.reshape(geo.heads, -1, part.shape[-1])
    values = lax.all_to_all(sent, "seq", split_axis=0, concat_axis=0, tiled=True)

    counts = jnp.sum(kept_all, axis=1) + block_count
    starts = jnp.cumsum(counts) - counts
    slot = (starts + (me - starts) % peers) // peers
    pick, last, key_tails, value_tails = plan(geo, slot, keys)
    packed_keys = unpack(geo, slot, keys, pick, last, key_tails)
    packed_values = unpack(geo, slot, values, pick, last, value_tails)

    sizes = kept_all.reshape(-1) + 1
    ends = jnp.cumsum(sizes)
    rank = jnp.arange(geo.slots, dtype=jnp.int32) * peers + me
    block = jnp.sum((rank[:, None] >= ends[None, :]).astype(jnp.int32), axis=1)
    folds = rank[:, None] == (ends - 1)[None, :]
    block_bias = jnp.log((BLOCK + 1 - sizes).astype(jnp.float32))
    packed_bias = jnp.sum(jnp.where(folds, block_bias[None, :], 0.0), axis=1).astype(jnp.bfloat16)
    owner = jnp.sum((block[:, None] >= request_ends[None, :]).astype(jnp.int32), axis=1)
    packed_request = jnp.where(rank < ends[-1], owner, -1)

    heads = geo.heads
    peak_score, softmax_total = part[..., HD], part[..., HD + LANES // 2]
    weighted = part[..., :HD]
    score_scale = 1.0 / jnp.sqrt(jnp.float32(HD))
    query_heads = queries.reshape(req_count, heads, HD)
    own_score = (
        jnp.einsum(
            "rhd,rhd->hr",
            query_heads,
            new_keys.reshape(req_count, heads, HD),
            preferred_element_type=jnp.float32,
        )
        * score_scale
    )
    final_peak = jnp.maximum(peak_score, own_score)
    rescale_old = jnp.exp(peak_score - final_peak)
    own_prob = jnp.exp(own_score - final_peak)
    new_value_heads = jnp.transpose(new_values.reshape(req_count, heads, HD), (1, 0, 2)).astype(
        jnp.float32
    )
    softmax_total = softmax_total * rescale_old + own_prob
    weighted = weighted * rescale_old[:, :, None] + own_prob[:, :, None] * new_value_heads
    attention_heads = weighted / softmax_total[:, :, None]
    attention = (
        jnp.transpose(attention_heads, (1, 0, 2))
        .reshape(req_count, heads * HD)
        .astype(jnp.bfloat16)
    )
    partial_output = jnp.dot(attention, out_weight, preferred_element_type=jnp.float32)
    layer_output = lax.psum_scatter(partial_output, "tp", scatter_dimension=0, tiled=True).astype(
        jnp.bfloat16
    )
    return (packed_keys, packed_values, packed_bias, packed_request, layer_output)


def solution(mesh):
    in_specs = (
        P("seq", "tp"),
        P("seq", "tp"),
        P("seq"),
        P("seq"),
        P(),
        P(None, "tp"),
        P(None, "tp"),
        P(None, "tp"),
        P("tp", "seq"),
    )
    out_specs = (P("seq", "tp"), P("seq", "tp"), P("seq"), P("seq"), P("tp", "seq"))
    return jax.shard_map(
        on_device, mesh=mesh, in_specs=in_specs, out_specs=out_specs, check_vma=False
    )
```
